32 devices in a mesh: dp: 32 (over z, y, x, core), tensor: 1.
Axes of the slice: x: 2, y: 2, z: 4, core: 2. Of those that a mesh axis runs over, the one named last changes fastest.
Arguments:
- user_feats: bfloat16 [4096, 1024], P(('dp', 'tensor')), may hold values from -240 to 240
- item_feats: bfloat16 [4096, 1024], P(('dp', 'tensor')), may hold values from -6 to 6
- user_w_in: bfloat16 [1024, 8192], P(None, 'tensor'), may hold values from -0.1875 to 0.1875
- user_w_out: bfloat16 [8192, 1024], P('tensor'), may hold values from -0.0625 to 0.0625
- item_w_in: bfloat16 [1024, 8192], P(None, 'tensor'), may hold values from -0.1875 to 0.1875
- item_w_out: bfloat16 [8192, 1024], P('tensor'), may hold values from -0.0625 to 0.0625
- teacher: float32 [4096, 2048], P(('dp', 'tensor')), may hold values from -250 to 250
- cand_blocks: int32 [32, 16], P(('dp', 'tensor')), may hold values from 0 to 31, all different within a row
- cand_count: int32 [32], P(('dp', 'tensor')), may hold values from 10 to 16
- owner_map: int32 [32], replicated, may hold values from 0 to 31, each once
Outputs:
- divergence: float32 [4096], P(('dp', 'tensor'))
- user_grad: float32 [4096, 1024], P(('dp', 'tensor'))
- item_grad: float32 [4096, 1024], P(('dp', 'tensor'))
The draws below stay inside these ranges and needn't reach their ends.
Inputs may be any that keep to these rules, and one draw needn't show every extreme that they name: `cand_blocks`: the 16 ids of one row are distinct. `owner_map`: every dp index appears exactly once.
All inputs are finite; a program needn't handle non-finite values.
Results may differ from the reference program's by a relative error of at most 0.017.
The reference program's roundings to bfloat16 on the way count: a program that leaves them out, or rounds other values in their place, can miss the bound.
Values may be sent and summed in bfloat16 or wider, within the bound.
No kernel may reach another device: no remote copies, remote signals or barrier semaphores. Data moves between devices by JAX's collectives and lax.ppermute only.
A program may use at most 128 MiB of HBM per device.

```python
import math
import jax
import jax.numpy as jnp
from jax import lax

D = 1024
FF = 8192
BLK = 128
K = 16
USERS = 4096
ITEMS = 4096
N_DP = 32
N_TENSOR = 1


def draw_user_feats(key, part):
    values = jnp.clip(jax.random.normal(key, (USERS, D), jnp.float32), -6.0, 6.0)
    return values.astype(jnp.bfloat16)


def draw_teacher(key, part):
    return jnp.clip(3.0 * jax.random.normal(key, (USERS, K * BLK), jnp.float32), -15.0, 15.0)


def plant(drawn, stream_key, low, largest):
    place = [jax.random.randint(jax.random.fold_in(stream_key, axis), (), 0, length) for axis, length in enumerate(drawn.shape)]
    longest = drawn.shape.index(max(drawn.shape))
    next_to = place[:longest] + [(place[longest] + 1) % drawn.shape[longest]] + place[longest + 1:]
    return drawn.at[tuple(place)].set(low).at[tuple(next_to)].set(largest)


def shard_levels(rng, extent, shards, least, largest):
    def one(axis_at, parts):
        draws = jax.random.uniform(jax.random.fold_in(jax.random.fold_in(rng, 6), axis_at), (parts,), jnp.float32, least / len(shards), largest / len(shards))
        return jnp.repeat(jnp.exp(draws), extent[axis_at] // parts).reshape((-1,) + (1,) * (len(extent) - axis_at - 1))

    factor_of = one(*shards[0])
    for cut in shards[1:]:
        factor_of = factor_of * one(*cut)
    return factor_of


def different_ones(stream_key, rows, amount, top, lift):
    order = jax.random.permutation(jax.random.fold_in(stream_key, 1), amount)
    favour = order
    for power in range(3):
        favour = favour * favour // amount
    favour = favour * lift // amount
    lots = jax.random.randint(jax.random.fold_in(stream_key, 2), (rows, amount), 0, 4096) + favour
    holders = jax.random.permutation(jax.random.fold_in(stream_key, 3), rows)[jnp.arange(amount) % rows]
    lots = jnp.where(jnp.arange(rows)[:, None] == holders[None, :], 1 << 14, lots)
    merit = lots * amount + jnp.arange(amount)
    return lax.top_k(merit.astype(jnp.int32), top)[1].astype(jnp.int32)


def bell_draw(stream_key, dims, spread, most, shards=(), held_as=jnp.bfloat16):
    factor_of = shard_levels(stream_key, dims, shards, -0.22, 0.18) if shards else 1.0
    entries = jax.random.normal(stream_key, dims, jnp.float32) * spread * factor_of
    return jnp.minimum(jnp.maximum(entries, -most), most).astype(held_as)


def setup_inputs(seed: int = 0) -> dict:
    splits = jax.random.split(jax.random.key(seed), 11)
    return {
        "user_feats": draw_user_feats(jax.random.fold_in(splits[10], 71), 0),
        "item_feats": bell_draw(splits[1], (ITEMS, D), 1.0, 6.0, ((0, 32),)),
        "user_w_in": bell_draw(splits[2], (D, FF), D ** -0.5, 0.1875),
        "user_w_out": bell_draw(splits[3], (FF, D), FF ** -0.5, 0.0625),
        "item_w_in": bell_draw(splits[4], (D, FF), D ** -0.5, 0.1875),
        "item_w_out": bell_draw(splits[5], (FF, D), FF ** -0.5, 0.0625),
        "teacher": draw_teacher(jax.random.fold_in(splits[10], 71), 0),
        "cand_blocks": different_ones(splits[7], (N_DP * N_TENSOR), N_DP, K, 8192),
        "cand_count": plant(jax.random.randint(splits[8], (N_DP * N_TENSOR,), 5 * K // 8, K + 1), jax.random.fold_in(splits[8], 1), 5 * K // 8, K).astype(jnp.int32),
        "owner_map": jax.random.permutation(splits[9], N_DP).astype(jnp.int32),
    }


def tower_apply(feats, w_in, w_out):

    def one_group(row_group):
        hidden = jax.nn.relu(jnp.dot(row_group, w_in, preferred_element_type=jnp.float32)).astype(jnp.bfloat16)
        return jnp.dot(hidden, w_out, preferred_element_type=jnp.float32).astype(jnp.bfloat16)
    grouped = feats.reshape(-1, BLK * N_TENSOR, feats.shape[1])
    return lax.map(one_group, grouped).reshape(feats.shape[0], w_out.shape[1])

def masked_softmax(logits, usable):
    highest = lax.optimization_barrier(jnp.max(jnp.where(usable, logits, -jnp.inf), axis=(1, 2), keepdims=True))
    shifted = jnp.where(usable, logits - highest, -jnp.inf)
    exponent = jnp.exp(shifted)
    denominator = lax.optimization_barrier(jnp.sum(exponent, axis=(1, 2), keepdims=True))
    log_prob = jnp.where(usable, shifted - jnp.log(denominator), 0.0)
    return (exponent / denominator, log_prob)

def reference(user_feats, item_feats, user_w_in, user_w_out, item_w_in, item_w_out, teacher, cand_blocks, cand_count, owner_map):
    user_emb = tower_apply(user_feats, user_w_in, user_w_out)
    item_emb = tower_apply(item_feats, item_w_in, item_w_out)
    item_blocks = item_emb.reshape(N_DP * N_TENSOR, BLK, D)
    user_blocks = user_emb.reshape(N_DP * N_TENSOR, BLK, D)
    teacher_blocks = teacher.reshape(N_DP * N_TENSOR, BLK, K, BLK)
    logit_scale = 3.0 / math.sqrt(D)
    loss_weight = BLK * K / 4.0

    def per_block(item_sums, scanned):
        block_index, user_rows, teacher_rows, candidates, live_count = scanned
        tensor_index = block_index % N_TENSOR
        targets = (owner_map[candidates] * N_TENSOR + tensor_index).astype(jnp.int32)
        picked = item_blocks[targets]
        student = logit_scale * jnp.einsum('ud,kjd->ukj', user_rows.astype(jnp.float32), picked.astype(jnp.float32))
        usable = (jnp.arange(K) < live_count)[None, :, None]
        teacher_prob, log_teacher = masked_softmax(teacher_rows, usable)
        student_prob, log_student = masked_softmax(student, usable)
        divergence = lax.optimization_barrier(jnp.sum(jnp.where(usable, teacher_prob * (log_teacher - log_student), 0.0), axis=(1, 2)))
        logit_grads = (loss_weight * logit_scale * (student_prob - teacher_prob)).astype(jnp.bfloat16)
        user_grad = jnp.einsum('ukj,kjd->ud', logit_grads.astype(jnp.float32), picked.astype(jnp.float32))
        contrib = jnp.einsum('ukj,ud->kjd', logit_grads.astype(jnp.float32), user_rows.astype(jnp.float32)).astype(jnp.bfloat16)
        item_sums = item_sums.at[targets].add(contrib.astype(jnp.float32))
        return (item_sums, (divergence, user_grad))
    start_sums = jnp.zeros((N_DP * N_TENSOR, BLK, D), jnp.float32)
    scanned = (jnp.arange(N_DP * N_TENSOR, dtype=jnp.int32), user_blocks, teacher_blocks, cand_blocks, cand_count)
    item_sums, (divergence, user_grad) = lax.scan(per_block, start_sums, scanned)
    return (divergence.reshape(-1), user_grad.reshape(-1, D), item_sums.reshape(-1, D))
```

```python
import functools
import math

import jax
import jax.numpy as jnp
from jax import lax
from jax.experimental import pallas as pl
from jax.experimental.pallas import tpu as pltpu
from jax.sharding import PartitionSpec as P

CORES = 2
DEAD = -1e30
LIVE = -1e29
MIB = 1 << 20
ANY = pl.BlockSpec(memory_space=pl.ANY)
VMEM = pl.BlockSpec(memory_space=pltpu.VMEM)
SMEM = pl.BlockSpec(memory_space=pltpu.SMEM)


def struct(shape, dtype):
    return jax.ShapeDtypeStruct(shape, dtype)


def params(mib):
    return pltpu.CompilerParams(vmem_limit_bytes=mib * MIB)


def cost(flops, moved):
    return pl.CostEstimate(flops=int(flops), bytes_accessed=int(moved), transcendentals=0)


def tower_body(chunks, feats, w_in, w_out, out, held_in, held_out, total, sem_in, sem_out):
    step = w_in.shape[1] // chunks

    def copies(i):
        part = pl.ds(pl.multiple_of(i * step, step), step)
        return (
            pltpu.make_async_copy(w_in.at[:, part], held_in.at[:, part], sem_in.at[i]),
            pltpu.make_async_copy(w_out.at[part], held_out.at[part], sem_out.at[i]),
        )

    for i in range(chunks):
        for copy in copies(i):
            copy.start()
    total[...] = jnp.zeros_like(total)

    def one(i, carry):
        first, second = copies(i)
        part = pl.ds(pl.multiple_of(i * step, step), step)
        first.wait()
        hidden = jnp.dot(feats[...], held_in[:, part], preferred_element_type=jnp.float32)
        hidden = jnp.maximum(hidden, 0.0).astype(jnp.bfloat16)
        second.wait()
        total[...] += jnp.dot(hidden, held_out[part], preferred_element_type=jnp.float32)
        return carry

    lax.fori_loop(0, chunks, one, 0)
    out[...] = total[...].astype(out.dtype)


def tower(feats, w_in, w_out, dtype):
    rows, width = feats.shape
    hidden = w_in.shape[1]
    chunks = max(1, hidden // 512)
    return pl.pallas_call(
        functools.partial(tower_body, chunks),
        in_specs=[VMEM, ANY, ANY],
        out_specs=VMEM,
        out_shape=struct((rows, width), dtype),
        scratch_shapes=[
            pltpu.VMEM(w_in.shape, w_in.dtype),
            pltpu.VMEM(w_out.shape, w_out.dtype),
            pltpu.VMEM((rows, width), jnp.float32),
            pltpu.SemaphoreType.DMA((chunks,)),
            pltpu.SemaphoreType.DMA((chunks,)),
        ],
        compiler_params=params(52),
        cost_estimate=cost(4 * rows * width * hidden, 4 * width * hidden),
    )(feats, w_in, w_out)


def embed(feats, w_in, w_out):
    if lax.axis_size("tensor") == 1:
        return tower(feats, w_in, w_out, jnp.bfloat16)
    feats = lax.all_gather(feats, "tensor", axis=0, tiled=True)
    partial = tower(feats, w_in, w_out, jnp.float32)
    return lax.psum_scatter(partial, "tensor", scatter_dimension=0, tiled=True).astype(jnp.bfloat16)


def teacher_body(cols, planes, me, cands, count, owner, teacher, *refs):
    places = CORES * cols
    outs, dense, sems = refs[:places], refs[places], refs[places + 1]
    rows = teacher.shape[0]
    slots = cands.shape[1]
    live = count[0]
    logits = teacher[...]
    usable = lax.broadcasted_iota(jnp.int32, logits.shape, 1) < live * rows
    shifted = logits - jnp.max(jnp.where(usable, logits, -jnp.inf), axis=1, keepdims=True)
    norm = jnp.sum(jnp.where(usable, jnp.exp(shifted), 0.0), axis=1, keepdims=True)
    log_p = shifted - jnp.log(norm)
    dense[...] = jnp.full(dense.shape, DEAD, jnp.float32)
    for k in range(slots):

        @pl.when(k < live)
        def _():
            apart = owner[cands[0, k]] ^ me[0]
            plane = apart // (CORES * cols)
            inside = apart % (CORES * cols)
            place = (inside % CORES) * cols + inside // CORES
            dense[place, plane] = log_p[:, k * rows : (k + 1) * rows].T

    copies = [pltpu.make_async_copy(dense.at[i], outs[i], sems.at[i]) for i in range(places)]
    for copy in copies:
        copy.start()
    for copy in copies:
        copy.wait()


def spread_teacher(cols, planes, me, cands, count, owner, teacher):
    rows = teacher.shape[0]
    places = CORES * cols
    return pl.pallas_call(
        functools.partial(teacher_body, cols, planes),
        in_specs=[SMEM, SMEM, SMEM, SMEM, VMEM],
        out_specs=[ANY] * places,
        out_shape=[struct((planes, rows, rows), jnp.float32)] * places,
        scratch_shapes=[
            pltpu.VMEM((places, planes, rows, rows), jnp.float32),
            pltpu.SemaphoreType.DMA((places,)),
        ],
        compiler_params=params(24),
        cost_estimate=cost(teacher.size, 8 * teacher.size),
    )(me, cands, count, owner, teacher)


def score_body(places, planes, scale, *refs):
    items, users, logs = refs[:planes], refs[planes : planes + places], refs[planes + places : planes + 2 * places]
    weights, stats, all_items, all_users, all_logs, item_sems, user_sems, log_sems = refs[planes + 2 * places :]
    rows = users[0].shape[0]
    load_items = [
        pltpu.make_async_copy(items[i], all_items.at[pl.ds(i * rows, rows)], item_sems.at[i]) for i in range(planes)
    ]
    load_users = [
        pltpu.make_async_copy(users[i], all_users.at[pl.ds(i * rows, rows)], user_sems.at[i]) for i in range(places)
    ]
    load_logs = [pltpu.make_async_copy(logs[i], all_logs.at[i], log_sems.at[i]) for i in range(places)]
    for copy in load_items:
        copy.start()
    for one, other in zip(load_users, load_logs):
        one.start()
        other.start()
    for copy in load_items:
        copy.wait()
    for first in range(0, places, 2):
        for i in (first, first + 1):
            load_users[i].wait()
            load_logs[i].wait()
        pair = pl.ds(first * rows, 2 * rows)
        both = scale * lax.dot_general(
            all_items[...], all_users[pair], (((1,), (1,)), ((), ())), preferred_element_type=jnp.float32
        )
        for j in (0, 1):
            score = both[:, j * rows : (j + 1) * rows]
            log_p = all_logs[first + j].reshape(planes * rows, rows)
            live = log_p > LIVE
            top = jnp.max(jnp.where(live, score, DEAD), axis=0, keepdims=True)
            shifted = score - top
            weight = jnp.where(live, jnp.exp(shifted), 0.0)
            prob = jnp.exp(log_p)
            weights[:, (first + j) * rows : (first + j + 1) * rows] = weight
            stats[0, first + j : first + j + 1, :] = top
            stats[1, first + j : first + j + 1, :] = jnp.sum(weight, axis=0, keepdims=True)
            stats[2, first + j : first + j + 1, :] = jnp.sum(
                jnp.where(live, prob * (log_p - shifted), 0.0), axis=0, keepdims=True
            )
            stats[3, first + j : first + j + 1, :] = jnp.sum(prob, axis=0, keepdims=True)


def scores(scale, items, users, logs):
    planes, places = len(items), len(users)
    rows, width = users[0].shape
    return pl.pallas_call(
        functools.partial(score_body, places, planes, scale),
        in_specs=[ANY] * (planes + 2 * places),
        out_specs=[VMEM, VMEM],
        out_shape=[
            struct((planes * rows, places * rows), jnp.float32),
            struct((4, places, rows), jnp.float32),
        ],
        scratch_shapes=[
            pltpu.VMEM((planes * rows, width), jnp.bfloat16),
            pltpu.VMEM((places * rows, width), jnp.bfloat16),
            pltpu.VMEM((places, planes, rows, rows), jnp.float32),
            pltpu.SemaphoreType.DMA((planes,)),
            pltpu.SemaphoreType.DMA((places,)),
            pltpu.SemaphoreType.DMA((places,)),
        ],
        compiler_params=params(32),
        cost_estimate=cost(2 * planes * places * rows * rows * width, 8 * planes * places * rows * rows),
    )(*items, *users, *logs)


def item_body(places, planes, factor, *refs):
    stats, users, logs = refs[:places], refs[places : 2 * places], refs[2 * places : 3 * places]
    weights, grads, divergence = refs[3 * places : 3 * places + 3]
    parts = refs[3 * places + 3 : 3 * places + 3 + planes]
    all_users, all_logs, user_sems, log_sems = refs[3 * places + 3 + planes :]
    rows = users[0].shape[0]
    load_users = [
        pltpu.make_async_copy(users[i], all_users.at[pl.ds(i * rows, rows)], user_sems.at[i]) for i in range(places)
    ]
    load_logs = [pltpu.make_async_copy(logs[i], all_logs.at[i], log_sems.at[i]) for i in range(places)]
    for copy in load_logs + load_users:
        copy.start()
    for i in range(places):
        tops = [stats[j][0, i ^ j : (i ^ j) + 1, :] for j in range(places)]
        sums = [stats[j][1, i ^ j : (i ^ j) + 1, :] for j in range(places)]
        top = functools.reduce(jnp.maximum, tops)
        norm = functools.reduce(jnp.add, [s * jnp.exp(t - top) for s, t in zip(sums, tops)])
        ratio = jnp.exp(tops[0] - top) / norm
        if i == 0:
            lse = top + jnp.log(norm)
            terms = [stats[j][2, j : j + 1, :] + stats[j][3, j : j + 1, :] * (lse - tops[j]) for j in range(places)]
            divergence[...] = functools.reduce(jnp.add, terms)
        load_logs[i].wait()
        prob = jnp.exp(all_logs[i].reshape(planes * rows, rows))
        lanes = slice(i * rows, (i + 1) * rows)
        grads[:, lanes] = (factor * (weights[:, lanes] * ratio - prob)).astype(jnp.bfloat16)
    for copy in load_users:
        copy.wait()
    for i in range(planes - 1, -1, -1):
        part = jnp.dot(grads[i * rows : (i + 1) * rows], all_users[...], preferred_element_type=jnp.float32)
        parts[i][...] = part.astype(parts[i].dtype)


def item_parts(factor, stats, users, logs, weights):
    places, planes = len(users), logs[0].shape[0]
    rows, width = users[0].shape
    return pl.pallas_call(
        functools.partial(item_body, places, planes, factor),
        in_specs=[VMEM] * places + [ANY] * (2 * places) + [VMEM],
        out_specs=[VMEM] * (2 + planes),
        out_shape=[struct(weights.shape, jnp.bfloat16), struct((1, rows), jnp.float32)]
        + [struct((rows, width), jnp.bfloat16 if i else jnp.float32) for i in range(planes)],
        scratch_shapes=[
            pltpu.VMEM((places * rows, width), jnp.bfloat16),
            pltpu.VMEM((places, planes, rows, rows), jnp.float32),
            pltpu.SemaphoreType.DMA((places,)),
            pltpu.SemaphoreType.DMA((places,)),
        ],
        compiler_params=params(32),
        cost_estimate=cost(2 * planes * places * rows * rows * width, 8 * planes * places * rows * rows),
    )(*stats, *users, *logs, weights)


def user_body(cols, planes, *refs):
    grads, items = refs[0], refs[1 : 1 + planes]
    own, other, all_items, sems = refs[1 + planes :]
    rows = items[0].shape[0]
    loads = [pltpu.make_async_copy(items[i], all_items.at[pl.ds(i * rows, rows)], sems.at[i]) for i in range(planes)]
    for copy in loads:
        copy.start()
    for copy in loads:
        copy.wait()
    half = cols * rows
    for i, out in enumerate((own, other)):
        out[...] = lax.dot_general(
            grads[:, i * half : (i + 1) * half],
            all_items[...],
            (((0,), (0,)), ((), ())),
            preferred_element_type=jnp.float32,
        ).astype(out.dtype)


def user_parts(cols, grads, items):
    planes = len(items)
    rows, width = items[0].shape
    return pl.pallas_call(
        functools.partial(user_body, cols, planes),
        in_specs=[VMEM] + [ANY] * planes,
        out_specs=[VMEM, VMEM],
        out_shape=[struct((cols * rows, width), jnp.float32), struct((cols * rows, width), jnp.bfloat16)],
        scratch_shapes=[pltpu.VMEM((planes * rows, width), jnp.bfloat16), pltpu.SemaphoreType.DMA((planes,))],
        compiler_params=params(32),
        cost_estimate=cost(2 * grads.size * width, 4 * grads.size),
    )(grads, *items)


def shards(
    user_feats, item_feats, user_w_in, user_w_out, item_w_in, item_w_out, teacher, cand_blocks, cand_count, owner_map
):
    rows, width = user_feats.shape
    slots = cand_blocks.shape[1]
    count = lax.axis_size("dp")
    cols = 1 << ((count // CORES).bit_length() - 1) // 2
    planes = count // (CORES * cols)
    assert cols * planes * CORES == count and count & (count - 1) == 0
    scale = 3.0 / math.sqrt(width)
    factor = rows * slots / 4.0 * scale
    me = lax.axis_index("dp")

    def swap(array, apart):
        return lax.ppermute(array, "dp", [(i, i ^ apart) for i in range(count)])

    def plane_apart(place):
        return (place % cols) * CORES + place // cols

    logs = spread_teacher(cols, planes, me.reshape(1).astype(jnp.int32), cand_blocks, cand_count, owner_map, teacher)
    item_feats, *logs = lax.optimization_barrier((item_feats, *logs))
    crossed = [swap(logs[cols + c], 1) for c in range(cols)]
    own_logs = [swap(logs[c], c * CORES) if c else logs[c] for c in range(cols)]
    other_logs = [swap(crossed[c], c * CORES) if c else crossed[c] for c in range(cols)]
    logs = own_logs + other_logs

    item_emb = embed(item_feats, item_w_in, item_w_out)
    user_feats, item_emb = lax.optimization_barrier((user_feats, item_emb))
    items = [item_emb] + [swap(item_emb, z * cols * CORES) for z in range(1, planes)]
    user_emb = embed(user_feats, user_w_in, user_w_out)
    users = [user_emb] + [swap(user_emb, c * CORES) for c in range(1, cols)]
    users = users + [swap(block, 1) for block in users]

    weights, stats = scores(scale, items, users, logs)
    all_stats = [stats] + [swap(stats, plane_apart(j)) for j in range(1, CORES * cols)]
    grads, divergence, *parts = item_parts(factor, all_stats, users, logs, weights)
    sent = [swap(parts[z], z * cols * CORES) for z in range(1, planes)]
    own, other = user_parts(cols, grads, items)
    half = (own + swap(other, 1).astype(jnp.float32)).reshape(cols, rows, width)
    arrived = [swap(half[c].astype(jnp.bfloat16), c * CORES) for c in range(1, cols)]

    def add(first, rest):
        return functools.reduce(jnp.add, [part.astype(jnp.float32) for part in rest], first)

    return (divergence.reshape(rows), add(half[0], arrived), add(parts[0], sent))


def solution(mesh):
    both = ("dp", "tensor")
    placed = (
        P(both, None),
        P(both, None),
        P(None, "tensor"),
        P("tensor", None),
        P(None, "tensor"),
        P("tensor", None),
        P(both, None),
        P(both, None),
        P(both),
        P(),
    )
    return jax.shard_map(
        shards,
        mesh=mesh,
        in_specs=placed,
        out_specs=(P(both), P(both, None), P(both, None)),
        check_vma=False,
    )
```

```python
import functools
import math

import jax
import jax.numpy as jnp
from jax import lax
from jax.experimental import pallas as pl
from jax.experimental.pallas import tpu as pltpu
from jax.sharding import PartitionSpec as P

CORES = 2
DEAD = -1e30
LIVE = -1e29
MIB = 1 << 20
ANY = pl.BlockSpec(memory_space=pl.ANY)
VMEM = pl.BlockSpec(memory_space=pltpu.VMEM)
SMEM = pl.BlockSpec(memory_space=pltpu.SMEM)


def struct(shape, dtype):
    return jax.ShapeDtypeStruct(shape, dtype)


def params(mib):
    return pltpu.CompilerParams(vmem_limit_bytes=mib * MIB)


def cost(flops, moved):
    return pl.CostEstimate(flops=int(flops), bytes_accessed=int(moved), transcendentals=0)


def tower_body(chunks, feats, w_in, w_out, *refs):
    out, held_in, held_out, total, sem_in, sem_out = refs[-6:]
    step = w_in.shape[1] // chunks

    def copies(i):
        part = pl.ds(pl.multiple_of(i * step, step), step)
        return (
            pltpu.make_async_copy(w_in.at[:, part], held_in.at[:, part], sem_in.at[i]),
            pltpu.make_async_copy(w_out.at[part], held_out.at[part], sem_out.at[i]),
        )

    for i in range(chunks):
        for copy in copies(i):
            copy.start()
    total[...] = jnp.zeros_like(total)

    def one(i, carry):
        first, second = copies(i)
        part = pl.ds(pl.multiple_of(i * step, step), step)
        first.wait()
        hidden = jnp.dot(feats[...], held_in[:, part], preferred_element_type=jnp.float32)
        hidden = jnp.maximum(hidden, 0.0).astype(jnp.bfloat16)
        second.wait()
        total[...] += jnp.dot(hidden, held_out[part], preferred_element_type=jnp.float32)
        return carry

    lax.fori_loop(0, chunks, one, 0)
    out[...] = total[...].astype(out.dtype)


def tower(feats, w_in, w_out, dtype, after):
    rows, width = feats.shape
    hidden = w_in.shape[1]
    chunks = max(1, hidden // 512)
    return pl.pallas_call(
        functools.partial(tower_body, chunks),
        in_specs=[VMEM, ANY, ANY] + [ANY] * len(after),
        out_specs=VMEM,
        out_shape=struct((rows, width), dtype),
        scratch_shapes=[
            pltpu.VMEM(w_in.shape, w_in.dtype),
            pltpu.VMEM(w_out.shape, w_out.dtype),
            pltpu.VMEM((rows, width), jnp.float32),
            pltpu.SemaphoreType.DMA((chunks,)),
            pltpu.SemaphoreType.DMA((chunks,)),
        ],
        compiler_params=params(52),
        cost_estimate=cost(1, 1),
    )(feats, w_in, w_out, *after)


def embed(feats, w_in, w_out, after):
    if lax.axis_size("tensor") == 1:
        return tower(feats, w_in, w_out, jnp.bfloat16, after)
    feats = lax.all_gather(feats, "tensor", axis=0, tiled=True)
    partial = tower(feats, w_in, w_out, jnp.float32, after)
    return lax.psum_scatter(partial, "tensor", scatter_dimension=0, tiled=True).astype(jnp.bfloat16)


def teacher_body(cols, planes, me, cands, count, owner, teacher, *refs):
    outs, dense, sems = refs[:cols], refs[cols], refs[cols + 1]
    rows = teacher.shape[0]
    slots = cands.shape[1]
    live = count[0]
    logits = teacher[...]
    usable = lax.broadcasted_iota(jnp.int32, logits.shape, 1) < live * rows
    shifted = logits - jnp.max(jnp.where(usable, logits, -jnp.inf), axis=1, keepdims=True)
    norm = jnp.sum(jnp.where(usable, jnp.exp(shifted), 0.0), axis=1, keepdims=True)
    log_p = shifted - jnp.log(norm)
    dense[...] = jnp.full(dense.shape, DEAD, jnp.float32)
    for k in range(slots):

        @pl.when(k < live)
        def _():
            apart = owner[cands[0, k]] ^ me[0]
            inside = apart % (CORES * cols)
            place = (inside % CORES) * planes + apart // (CORES * cols)
            dense[inside // CORES, place] = log_p[:, k * rows : (k + 1) * rows].T

    copies = [pltpu.make_async_copy(dense.at[i], outs[i], sems.at[i]) for i in range(cols)]
    for copy in copies:
        copy.start()
    for copy in copies:
        copy.wait()


def spread_teacher(cols, planes, me, cands, count, owner, teacher):
    rows = teacher.shape[0]
    places = CORES * planes
    return pl.pallas_call(
        functools.partial(teacher_body, cols, planes),
        in_specs=[SMEM, SMEM, SMEM, SMEM, VMEM],
        out_specs=[ANY] * cols,
        out_shape=[struct((places, rows, rows), jnp.float32)] * cols,
        scratch_shapes=[
            pltpu.VMEM((cols, places, rows, rows), jnp.float32),
            pltpu.SemaphoreType.DMA((cols,)),
        ],
        compiler_params=params(24),
        cost_estimate=cost(teacher.size, 8 * teacher.size),
    )(me, cands, count, owner, teacher)


def loads_of(sources, target, sems):
    rows = sources[0].shape[0]
    return [
        pltpu.make_async_copy(source, target.at[pl.ds(i * rows, rows)], sems.at[i]) for i, source in enumerate(sources)
    ]


def score_body(cols, places, scale, *refs):
    users, items, logs = refs[:cols], refs[cols : cols + places], refs[cols + places : 2 * cols + places]
    weights, stats, all_users, all_items, all_logs, user_sems, item_sems, log_sems = refs[2 * cols + places :]
    rows = users[0].shape[0]
    load_users = loads_of(users, all_users, user_sems)
    load_items = loads_of(items, all_items, item_sems)
    load_logs = loads_of(logs, all_logs, log_sems)
    for copy in load_items + load_users + load_logs:
        copy.start()
    for copy in load_items:
        copy.wait()
    step = 2 if cols % 2 == 0 else 1
    for first in range(0, cols, step):
        for i in range(first, first + step):
            load_users[i].wait()
        both = scale * lax.dot_general(
            all_items[...],
            all_users[first * rows : (first + step) * rows],
            (((1,), (1,)), ((), ())),
            preferred_element_type=jnp.float32,
        )
        for j in range(step):
            i = first + j
            load_logs[i].wait()
            score = both[:, j * rows : (j + 1) * rows]
            log_p = all_logs[i * places : (i + 1) * places].reshape(places * rows, rows)
            live = log_p > LIVE
            top = jnp.max(jnp.where(live, score, DEAD), axis=0, keepdims=True)
            shifted = score - top
            weight = jnp.where(live, jnp.exp(shifted), 0.0)
            prob = jnp.exp(log_p)
            weights[:, i * rows : (i + 1) * rows] = weight
            stats[0, i : i + 1, :] = top
            stats[1, i : i + 1, :] = jnp.sum(weight, axis=0, keepdims=True)
            stats[2, i : i + 1, :] = jnp.sum(jnp.where(live, prob * (log_p - shifted), 0.0), axis=0, keepdims=True)
            stats[3, i : i + 1, :] = jnp.sum(prob, axis=0, keepdims=True)


def scores(scale, users, items, logs):
    cols, places = len(users), len(items)
    rows, width = users[0].shape
    return pl.pallas_call(
        functools.partial(score_body, cols, places, scale),
        in_specs=[ANY] * (2 * cols + places),
        out_specs=[VMEM, VMEM],
        out_shape=[
            struct((places * rows, cols * rows), jnp.float32),
            struct((4, cols, rows), jnp.float32),
        ],
        scratch_shapes=[
            pltpu.VMEM((cols * rows, width), jnp.bfloat16),
            pltpu.VMEM((places * rows, width), jnp.bfloat16),
            pltpu.VMEM((cols * places, rows, rows), jnp.float32),
            pltpu.SemaphoreType.DMA((cols,)),
            pltpu.SemaphoreType.DMA((places,)),
            pltpu.SemaphoreType.DMA((cols,)),
        ],
        compiler_params=params(32),
        cost_estimate=cost(2 * cols * places * rows * rows * width, 8 * cols * places * rows * rows),
    )(*users, *items, *logs)


def far_body(cols, places, factor, *refs):
    stats, users, logs = refs[:cols], refs[cols : 2 * cols], refs[2 * cols : 3 * cols]
    weights, grads, divergence, far = refs[3 * cols : 3 * cols + 4]
    all_users, all_logs, user_sems, log_sems = refs[3 * cols + 4 :]
    rows = users[0].shape[0]
    load_users = loads_of(users, all_users, user_sems)
    load_logs = loads_of(logs, all_logs, log_sems)
    for copy in load_logs + load_users:
        copy.start()
    for i in range(cols):
        tops = [stats[j][0, i ^ j : (i ^ j) + 1, :] for j in range(cols)]
        sums = [stats[j][1, i ^ j : (i ^ j) + 1, :] for j in range(cols)]
        top = functools.reduce(jnp.maximum, tops)
        norm = functools.reduce(jnp.add, [s * jnp.exp(t - top) for s, t in zip(sums, tops)])
        ratio = jnp.exp(tops[0] - top) / norm
        if i == 0:
            lse = top + jnp.log(norm)
            terms = [stats[j][2, j : j + 1, :] + stats[j][3, j : j + 1, :] * (lse - tops[j]) for j in range(cols)]
            divergence[...] = functools.reduce(jnp.add, terms)
        load_logs[i].wait()
        prob = jnp.exp(all_logs[i * places : (i + 1) * places].reshape(places * rows, rows))
        lanes = slice(i * rows, (i + 1) * rows)
        grads[:, lanes] = (factor * (weights[:, lanes] * ratio - prob)).astype(jnp.bfloat16)
    for copy in load_users:
        copy.wait()
    half = places * rows // CORES
    far[...] = jnp.dot(grads[half:], all_users[...], preferred_element_type=jnp.float32).astype(far.dtype)


def far_parts(factor, stats, users, logs, weights):
    cols, places = len(users), logs[0].shape[0]
    rows, width = users[0].shape
    return pl.pallas_call(
        functools.partial(far_body, cols, places, factor),
        in_specs=[VMEM] * cols + [ANY] * (2 * cols) + [VMEM],
        out_specs=[VMEM] * 3,
        out_shape=[
            struct(weights.shape, jnp.bfloat16),
            struct((1, rows), jnp.float32),
            struct((places * rows // CORES, width), jnp.bfloat16),
        ],
        scratch_shapes=[
            pltpu.VMEM((cols * rows, width), jnp.bfloat16),
            pltpu.VMEM((cols * places, rows, rows), jnp.float32),
            pltpu.SemaphoreType.DMA((cols,)),
            pltpu.SemaphoreType.DMA((cols,)),
        ],
        compiler_params=params(32),
        cost_estimate=cost(cols * places * rows * rows * width, 8 * cols * places * rows * rows),
    )(*stats, *users, *logs, weights)


def near_body(cols, places, *refs):
    grads, users, items = refs[0], refs[1 : 1 + cols], refs[1 + cols : 1 + cols + places]
    near = refs[1 + cols + places]
    parts = refs[2 + cols + places : 2 + 2 * cols + places]
    all_users, all_items, user_sems, item_sems = refs[2 + 2 * cols + places :]
    rows = users[0].shape[0]
    load_users = loads_of(users, all_users, user_sems)
    load_items = loads_of(items, all_items, item_sems)
    for copy in load_users + load_items:
        copy.start()
    for copy in load_users:
        copy.wait()
    half = places * rows // CORES
    near[...] = jnp.dot(grads[:half], all_users[...], preferred_element_type=jnp.float32)
    for copy in load_items:
        copy.wait()
    for i in range(cols):
        part = lax.dot_general(
            grads[:, i * rows : (i + 1) * rows],
            all_items[...],
            (((0,), (0,)), ((), ())),
            preferred_element_type=jnp.float32,
        )
        parts[i][...] = part.astype(parts[i].dtype)


def near_parts(grads, users, items):
    cols, places = len(users), len(items)
    rows, width = users[0].shape
    return pl.pallas_call(
        functools.partial(near_body, cols, places),
        in_specs=[VMEM] + [ANY] * (cols + places),
        out_specs=[VMEM] * (1 + cols),
        out_shape=[struct((places * rows // CORES, width), jnp.float32)]
        + [struct((rows, width), jnp.bfloat16 if i else jnp.float32) for i in range(cols)],
        scratch_shapes=[
            pltpu.VMEM((cols * rows, width), jnp.bfloat16),
            pltpu.VMEM((places * rows, width), jnp.bfloat16),
            pltpu.SemaphoreType.DMA((cols,)),
            pltpu.SemaphoreType.DMA((places,)),
        ],
        compiler_params=params(32),
        cost_estimate=cost(3 * cols * places * rows * rows * width, 8 * cols * places * rows * rows),
    )(grads, *users, *items)


def join_body(planes, near, far, *outs):
    rows = outs[0].shape[0]
    for i in range(planes - 1, -1, -1):
        part = slice(i * rows, (i + 1) * rows)
        outs[i][...] = (near[part] + far[part].astype(jnp.float32)).astype(outs[i].dtype)


def join(planes, near, far):
    rows, width = near.shape[0] // planes, near.shape[1]
    return pl.pallas_call(
        functools.partial(join_body, planes),
        in_specs=[VMEM, VMEM],
        out_specs=[VMEM] * planes,
        out_shape=[struct((rows, width), jnp.bfloat16 if i else jnp.float32) for i in range(planes)],
        compiler_params=params(24),
        cost_estimate=cost(near.size, 8 * near.size),
    )(near, far)


def shards(
    user_feats, item_feats, user_w_in, user_w_out, item_w_in, item_w_out, teacher, cand_blocks, cand_count, owner_map
):
    rows, width = user_feats.shape
    slots = cand_blocks.shape[1]
    count = lax.axis_size("dp")
    cols = 1 << ((count // CORES).bit_length() - 1) // 2
    planes = count // (CORES * cols)
    assert cols * planes * CORES == count and count & (count - 1) == 0
    scale = 3.0 / math.sqrt(width)
    factor = rows * slots / 4.0 * scale
    me = lax.axis_index("dp").reshape(1).astype(jnp.int32)

    def swap(array, apart):
        return lax.ppermute(array, "dp", [(i, i ^ apart) for i in range(count)])

    def over_columns(own):
        return [swap(own, c * CORES) for c in range(1, cols)]

    logs = spread_teacher(cols, planes, me, cand_blocks, cand_count, owner_map, teacher)
    first, *rest = logs
    logs = [first] + [swap(part, (c + 1) * CORES) for c, part in enumerate(rest)]

    item_emb = embed(item_feats, item_w_in, item_w_out, [first])
    wide = planes // 2
    crossed = [swap(item_emb, z * cols * CORES) for z in range(wide, planes if planes > 1 else 0, max(wide, 1))]
    nearby = [swap(item_emb, z * cols * CORES) for z in range(1, wide)]
    user_emb = embed(user_feats, user_w_in, user_w_out, [item_emb])
    user_emb, item_emb, logs, crossed, nearby = lax.optimization_barrier((user_emb, item_emb, logs, crossed, nearby))
    users = [user_emb] + over_columns(user_emb)
    items = [item_emb] + nearby + crossed + [swap(block, z * cols * CORES) for block in crossed for z in range(1, wide)]
    items = items + [swap(block, 1) for block in items]

    weights, stats = scores(scale, users, items, logs)
    grads, divergence, far = far_parts(factor, [stats] + over_columns(stats), users, logs, weights)
    far = swap(far, 1)
    near, own, *others = near_parts(grads, users, items)
    arrived = [swap(part, (c + 1) * CORES) for c, part in enumerate(others)]
    parts = join(planes, near, far)
    sent = [swap(parts[z], z * cols * CORES) for z in range(planes - 1, 0, -1)]

    def add(start, parts):
        return functools.reduce(jnp.add, [part.astype(jnp.float32) for part in parts], start)

    return (divergence.reshape(rows), add(own, arrived), add(parts[0], sent))


def solution(mesh):
    both = ("dp", "tensor")
    placed = (
        P(both, None),
        P(both, None),
        P(None, "tensor"),
        P("tensor", None),
        P(None, "tensor"),
        P("tensor", None),
        P(both, None),
        P(both, None),
        P(both),
        P(),
    )
    return jax.shard_map(
        shards,
        mesh=mesh,
        in_specs=placed,
        out_specs=(P(both), P(both, None), P(both, None)),
        check_vma=False,
    )
```

```python
import functools
import math

import jax
import jax.numpy as jnp
from jax import lax
from jax.experimental import pallas as pl
from jax.experimental.pallas import tpu as pltpu
from jax.sharding import PartitionSpec as P

CORES = 2
DEAD = -1e30
LIVE = -1e29
MIB = 1 << 20
ANY = pl.BlockSpec(memory_space=pl.ANY)
VMEM = pl.BlockSpec(memory_space=pltpu.VMEM)
SMEM = pl.BlockSpec(memory_space=pltpu.SMEM)


def struct(shape, dtype):
    return jax.ShapeDtypeStruct(shape, dtype)


def params(mib):
    return pltpu.CompilerParams(vmem_limit_bytes=mib * MIB)


def cost(flops, moved):
    return pl.CostEstimate(flops=int(flops), bytes_accessed=int(moved), transcendentals=0)


def tower_body(chunks, feats, w_in, w_out, *refs):
    out, held_in, held_out, total, sem_in, sem_out = refs[-6:]
    step = w_in.shape[1] // chunks

    def copies(i):
        part = pl.ds(pl.multiple_of(i * step, step), step)
        return (
            pltpu.make_async_copy(w_in.at[:, part], held_in.at[:, part], sem_in.at[i]),
            pltpu.make_async_copy(w_out.at[part], held_out.at[part], sem_out.at[i]),
        )

    for i in range(chunks):
        for copy in copies(i):
            copy.start()
    total[...] = jnp.zeros_like(total)

    def one(i, carry):
        first, second = copies(i)
        part = pl.ds(pl.multiple_of(i * step, step), step)
        first.wait()
        hidden = jnp.dot(feats[...], held_in[:, part], preferred_element_type=jnp.float32)
        hidden = jnp.maximum(hidden, 0.0).astype(jnp.bfloat16)
        second.wait()
        total[...] += jnp.dot(hidden, held_out[part], preferred_element_type=jnp.float32)
        return carry

    lax.fori_loop(0, chunks, one, 0)
    out[...] = total[...].astype(out.dtype)


def tower(feats, w_in, w_out, dtype, after):
    rows, width = feats.shape
    hidden = w_in.shape[1]
    chunks = max(1, hidden // 512)
    return pl.pallas_call(
        functools.partial(tower_body, chunks),
        in_specs=[VMEM, ANY, ANY] + [ANY] * len(after),
        out_specs=VMEM,
        out_shape=struct((rows, width), dtype),
        scratch_shapes=[
            pltpu.VMEM(w_in.shape, w_in.dtype),
            pltpu.VMEM(w_out.shape, w_out.dtype),
            pltpu.VMEM((rows, width), jnp.float32),
            pltpu.SemaphoreType.DMA((chunks,)),
            pltpu.SemaphoreType.DMA((chunks,)),
        ],
        compiler_params=params(52),
        cost_estimate=cost(1, 1),
    )(feats, w_in, w_out, *after)


def embed(feats, w_in, w_out, after):
    if lax.axis_size("tensor") == 1:
        return tower(feats, w_in, w_out, jnp.bfloat16, after)
    feats = lax.all_gather(feats, "tensor", axis=0, tiled=True)
    partial = tower(feats, w_in, w_out, jnp.float32, after)
    return lax.psum_scatter(partial, "tensor", scatter_dimension=0, tiled=True).astype(jnp.bfloat16)


def teacher_body(cols, planes, me, cands, count, owner, teacher, *refs):
    outs, dense, sems = refs[:cols], refs[cols], refs[cols + 1]
    rows = teacher.shape[0]
    slots = cands.shape[1]
    live = count[0]
    logits = teacher[...]
    usable = lax.broadcasted_iota(jnp.int32, logits.shape, 1) < live * rows
    shifted = logits - jnp.max(jnp.where(usable, logits, -jnp.inf), axis=1, keepdims=True)
    norm = jnp.sum(jnp.where(usable, jnp.exp(shifted), 0.0), axis=1, keepdims=True)
    log_p = shifted - jnp.log(norm)
    dense[...] = jnp.full(dense.shape, DEAD, jnp.float32)
    for k in range(slots):

        @pl.when(k < live)
        def _():
            apart = owner[cands[0, k]] ^ me[0]
            inside = apart % (CORES * cols)
            place = (inside % CORES) * planes + apart // (CORES * cols)
            dense[inside // CORES, place] = log_p[:, k * rows : (k + 1) * rows].T

    copies = [pltpu.make_async_copy(dense.at[i], outs[i], sems.at[i]) for i in range(cols)]
    for copy in copies:
        copy.start()
    for copy in copies:
        copy.wait()


def spread_teacher(cols, planes, me, cands, count, owner, teacher):
    rows = teacher.shape[0]
    places = CORES * planes
    return pl.pallas_call(
        functools.partial(teacher_body, cols, planes),
        in_specs=[SMEM, SMEM, SMEM, SMEM, VMEM],
        out_specs=[ANY] * cols,
        out_shape=[struct((places, rows, rows), jnp.float32)] * cols,
        scratch_shapes=[
            pltpu.VMEM((cols, places, rows, rows), jnp.float32),
            pltpu.SemaphoreType.DMA((cols,)),
        ],
        compiler_params=params(24),
        cost_estimate=cost(teacher.size, 8 * teacher.size),
    )(me, cands, count, owner, teacher)


def loads_of(sources, target, sems):
    rows = sources[0].shape[0]
    return [
        pltpu.make_async_copy(source, target.at[pl.ds(i * rows, rows)], sems.at[i]) for i, source in enumerate(sources)
    ]


def score_body(cols, places, scale, *refs):
    users, items, logs = refs[:cols], refs[cols : cols + places], refs[cols + places : 2 * cols + places]
    weights, stats, all_users, all_items, all_logs, user_sems, item_sems, log_sems = refs[2 * cols + places :]
    rows = users[0].shape[0]
    load_users = loads_of(users, all_users, user_sems)
    load_items = loads_of(items, all_items, item_sems)
    load_logs = loads_of(logs, all_logs, log_sems)
    for copy in load_items + load_users + load_logs:
        copy.start()
    for copy in load_items:
        copy.wait()
    step = 2 if cols % 2 == 0 else 1
    for first in range(0, cols, step):
        for i in range(first, first + step):
            load_users[i].wait()
        both = scale * lax.dot_general(
            all_items[...],
            all_users[first * rows : (first + step) * rows],
            (((1,), (1,)), ((), ())),
            preferred_element_type=jnp.float32,
        )
        for j in range(step):
            i = first + j
            load_logs[i].wait()
            score = both[:, j * rows : (j + 1) * rows]
            log_p = all_logs[i * places : (i + 1) * places].reshape(places * rows, rows)
            live = log_p > LIVE
            top = jnp.max(jnp.where(live, score, DEAD), axis=0, keepdims=True)
            shifted = score - top
            weight = jnp.where(live, jnp.exp(shifted), 0.0)
            prob = jnp.exp(log_p)
            weights[:, i * rows : (i + 1) * rows] = weight
            stats[0, i : i + 1, :] = top
            stats[1, i : i + 1, :] = jnp.sum(weight, axis=0, keepdims=True)
            stats[2, i : i + 1, :] = jnp.sum(jnp.where(live, prob * (log_p - shifted), 0.0), axis=0, keepdims=True)
            stats[3, i : i + 1, :] = jnp.sum(prob, axis=0, keepdims=True)


def scores(scale, users, items, logs):
    cols, places = len(users), len(items)
    rows, width = users[0].shape
    return pl.pallas_call(
        functools.partial(score_body, cols, places, scale),
        in_specs=[ANY] * (2 * cols + places),
        out_specs=[VMEM, VMEM],
        out_shape=[
            struct((places * rows, cols * rows), jnp.float32),
            struct((4, cols, rows), jnp.float32),
        ],
        scratch_shapes=[
            pltpu.VMEM((cols * rows, width), jnp.bfloat16),
            pltpu.VMEM((places * rows, width), jnp.bfloat16),
            pltpu.VMEM((cols * places, rows, rows), jnp.float32),
            pltpu.SemaphoreType.DMA((cols,)),
            pltpu.SemaphoreType.DMA((places,)),
            pltpu.SemaphoreType.DMA((cols,)),
        ],
        compiler_params=params(32),
        cost_estimate=cost(2 * cols * places * rows * rows * width, 8 * cols * places * rows * rows),
    )(*users, *items, *logs)


def far_body(cols, places, factor, *refs):
    stats, users, logs = refs[:cols], refs[cols : 2 * cols], refs[2 * cols : 3 * cols]
    weights, grads, divergence, far = refs[3 * cols : 3 * cols + 4]
    all_users, all_logs, user_sems, log_sems = refs[3 * cols + 4 :]
    rows = users[0].shape[0]
    load_users = loads_of(users, all_users, user_sems)
    load_logs = loads_of(logs, all_logs, log_sems)
    for copy in load_logs + load_users:
        copy.start()
    for i in range(cols):
        tops = [stats[j][0, i ^ j : (i ^ j) + 1, :] for j in range(cols)]
        sums = [stats[j][1, i ^ j : (i ^ j) + 1, :] for j in range(cols)]
        top = functools.reduce(jnp.maximum, tops)
        norm = functools.reduce(jnp.add, [s * jnp.exp(t - top) for s, t in zip(sums, tops)])
        ratio = jnp.exp(tops[0] - top) / norm
        if i == 0:
            lse = top + jnp.log(norm)
            terms = [stats[j][2, j : j + 1, :] + stats[j][3, j : j + 1, :] * (lse - tops[j]) for j in range(cols)]
            divergence[...] = functools.reduce(jnp.add, terms)
        load_logs[i].wait()
        prob = jnp.exp(all_logs[i * places : (i + 1) * places].reshape(places * rows, rows))
        lanes = slice(i * rows, (i + 1) * rows)
        grads[:, lanes] = (factor * (weights[:, lanes] * ratio - prob)).astype(jnp.bfloat16)
    for copy in load_users:
        copy.wait()
    half = places * rows // CORES
    far[...] = jnp.dot(grads[half:], all_users[...], preferred_element_type=jnp.float32).astype(far.dtype)


def far_parts(factor, stats, users, logs, weights):
    cols, places = len(users), logs[0].shape[0]
    rows, width = users[0].shape
    return pl.pallas_call(
        functools.partial(far_body, cols, places, factor),
        in_specs=[VMEM] * cols + [ANY] * (2 * cols) + [VMEM],
        out_specs=[VMEM] * 3,
        out_shape=[
            struct(weights.shape, jnp.bfloat16),
            struct((1, rows), jnp.float32),
            struct((places * rows // CORES, width), jnp.bfloat16),
        ],
        scratch_shapes=[
            pltpu.VMEM((cols * rows, width), jnp.bfloat16),
            pltpu.VMEM((cols * places, rows, rows), jnp.float32),
            pltpu.SemaphoreType.DMA((cols,)),
            pltpu.SemaphoreType.DMA((cols,)),
        ],
        compiler_params=params(32),
        cost_estimate=cost(cols * places * rows * rows * width, 8 * cols * places * rows * rows),
    )(*stats, *users, *logs, weights)


def near_body(cols, grads, *refs):
    users, (near, all_users, sems) = refs[:cols], refs[cols:]
    loads = loads_of(users, all_users, sems)
    for copy in loads:
        copy.start()
    for copy in loads:
        copy.wait()
    near[...] = jnp.dot(grads[: near.shape[0]], all_users[...], preferred_element_type=jnp.float32)


def near_part(grads, users):
    cols, places = len(users), grads.shape[0]
    rows, width = users[0].shape
    return pl.pallas_call(
        functools.partial(near_body, cols),
        in_specs=[VMEM] + [ANY] * cols,
        out_specs=VMEM,
        out_shape=struct((places // CORES, width), jnp.float32),
        scratch_shapes=[pltpu.VMEM((cols * rows, width), jnp.bfloat16), pltpu.SemaphoreType.DMA((cols,))],
        compiler_params=params(32),
        cost_estimate=cost(grads.size * width, 4 * grads.size),
    )(grads, *users)


def user_body(cols, places, grads, *refs):
    items, refs = refs[:places], refs[-cols - 2 :]
    parts, (all_items, sems) = refs[:cols], refs[cols:]
    rows = items[0].shape[0]
    loads = loads_of(items, all_items, sems)
    for copy in loads:
        copy.start()
    for copy in loads:
        copy.wait()
    for i in range(cols - 1, -1, -1):
        part = lax.dot_general(
            grads[:, i * rows : (i + 1) * rows],
            all_items[...],
            (((0,), (0,)), ((), ())),
            preferred_element_type=jnp.float32,
        )
        parts[i][...] = part.astype(parts[i].dtype)


def user_parts(cols, grads, items, after):
    places = len(items)
    rows, width = items[0].shape
    return pl.pallas_call(
        functools.partial(user_body, cols, places),
        in_specs=[VMEM] + [ANY] * (places + len(after)),
        out_specs=[VMEM] * cols,
        out_shape=[struct((rows, width), jnp.bfloat16 if i else jnp.float32) for i in range(cols)],
        scratch_shapes=[pltpu.VMEM((places * rows, width), jnp.bfloat16), pltpu.SemaphoreType.DMA((places,))],
        compiler_params=params(32),
        cost_estimate=cost(2 * grads.size * width, 4 * grads.size),
    )(grads, *items, *after)


def join_body(planes, near, far, *outs):
    rows = outs[0].shape[0]
    for i in range(planes - 1, -1, -1):
        part = slice(i * rows, (i + 1) * rows)
        outs[i][...] = (near[part] + far[part].astype(jnp.float32)).astype(outs[i].dtype)


def join(planes, near, far):
    rows, width = near.shape[0] // planes, near.shape[1]
    return pl.pallas_call(
        functools.partial(join_body, planes),
        in_specs=[VMEM, VMEM],
        out_specs=[VMEM] * planes,
        out_shape=[struct((rows, width), jnp.bfloat16 if i else jnp.float32) for i in range(planes)],
        compiler_params=params(24),
        cost_estimate=cost(near.size, 8 * near.size),
    )(near, far)


def shards(
    user_feats, item_feats, user_w_in, user_w_out, item_w_in, item_w_out, teacher, cand_blocks, cand_count, owner_map
):
    rows, width = user_feats.shape
    slots = cand_blocks.shape[1]
    count = lax.axis_size("dp")
    cols = 1 << ((count // CORES).bit_length() - 1) // 2
    planes = count // (CORES * cols)
    assert cols * planes * CORES == count and count & (count - 1) == 0
    scale = 3.0 / math.sqrt(width)
    factor = rows * slots / 4.0 * scale
    me = lax.axis_index("dp").reshape(1).astype(jnp.int32)

    def swap(array, apart):
        return lax.ppermute(array, "dp", [(i, i ^ apart) for i in range(count)])

    def over_columns(own):
        return [swap(own, c * CORES) for c in range(1, cols)]

    logs = spread_teacher(cols, planes, me, cand_blocks, cand_count, owner_map, teacher)
    first, *rest = logs
    logs = [first] + [swap(part, (c + 1) * CORES) for c, part in enumerate(rest)]

    item_emb = embed(item_feats, item_w_in, item_w_out, [first])
    wide = planes // 2
    crossed = [swap(item_emb, z * cols * CORES) for z in range(wide, planes if planes > 1 else 0, max(wide, 1))]
    nearby = [swap(item_emb, z * cols * CORES) for z in range(1, wide)]
    user_emb = embed(user_feats, user_w_in, user_w_out, [item_emb])
    user_emb, item_emb, logs, crossed, nearby = lax.optimization_barrier((user_emb, item_emb, logs, crossed, nearby))
    users = [user_emb] + over_columns(user_emb)
    derived = [swap(block, z * cols * CORES) for block in crossed for z in range(1, wide)]
    if cols > 1:
        users[1], item_emb, nearby, crossed = lax.optimization_barrier((users[1], item_emb, nearby, crossed))
    items = [item_emb] + nearby + crossed + derived
    items = items + [swap(block, 1) for block in items]

    weights, stats = scores(scale, users, items, logs)
    grads, divergence, far = far_parts(factor, [stats] + over_columns(stats), users, logs, weights)
    far = swap(far, 1)
    parts = join(planes, near_part(grads, users), far)
    sent = [swap(parts[z], z * cols * CORES) for z in range(planes - 1, 0, -1)]
    own, *others = user_parts(cols, grads, items, [parts[0]])
    arrived = [swap(part, (c + 1) * CORES) for c, part in enumerate(others)]

    def add(start, parts):
        return functools.reduce(jnp.add, [part.astype(jnp.float32) for part in parts], start)

    return (divergence.reshape(rows), add(own, arrived), add(parts[0], sent))


def solution(mesh):
    both = ("dp", "tensor")
    placed = (
        P(both, None),
        P(both, None),
        P(None, "tensor"),
        P("tensor", None),
        P(None, "tensor"),
        P("tensor", None),
        P(both, None),
        P(both, None),
        P(both),
        P(),
    )
    return jax.shard_map(
        shards,
        mesh=mesh,
        in_specs=placed,
        out_specs=(P(both), P(both, None), P(both, None)),
        check_vma=False,
    )
```

```python
import functools
import math

import jax
import jax.numpy as jnp
from jax import lax
from jax.experimental import pallas as pl
from jax.experimental.pallas import tpu as pltpu
from jax.sharding import PartitionSpec as P

CORES = 2
DEAD = -1e30
LIVE = -1e29
MIB = 1 << 20
ANY = pl.BlockSpec(memory_space=pl.ANY)
VMEM = pl.BlockSpec(memory_space=pltpu.VMEM)
SMEM = pl.BlockSpec(memory_space=pltpu.SMEM)


def struct(shape, dtype):
    return jax.ShapeDtypeStruct(shape, dtype)


def params(mib):
    return pltpu.CompilerParams(vmem_limit_bytes=mib * MIB)


def cost(flops, moved):
    return pl.CostEstimate(flops=int(flops), bytes_accessed=int(moved), transcendentals=0)


def tower_body(chunks, feats, w_in, w_out, *refs):
    out, held_in, held_out, total, sem_in, sem_out = refs[-6:]
    step = w_in.shape[1] // chunks

    def copies(i):
        part = pl.ds(pl.multiple_of(i * step, step), step)
        return (
            pltpu.make_async_copy(w_in.at[:, part], held_in.at[:, part], sem_in.at[i]),
            pltpu.make_async_copy(w_out.at[part], held_out.at[part], sem_out.at[i]),
        )

    for i in range(chunks):
        for copy in copies(i):
            copy.start()
    total[...] = jnp.zeros_like(total)

    def one(i, carry):
        first, second = copies(i)
        part = pl.ds(pl.multiple_of(i * step, step), step)
        first.wait()
        hidden = jnp.dot(feats[...], held_in[:, part], preferred_element_type=jnp.float32)
        hidden = jnp.maximum(hidden, 0.0).astype(jnp.bfloat16)
        second.wait()
        total[...] += jnp.dot(hidden, held_out[part], preferred_element_type=jnp.float32)
        return carry

    lax.fori_loop(0, chunks, one, 0)
    out[...] = total[...].astype(out.dtype)


def tower(feats, w_in, w_out, dtype, after):
    rows, width = feats.shape
    hidden = w_in.shape[1]
    chunks = max(1, hidden // 512)
    return pl.pallas_call(
        functools.partial(tower_body, chunks),
        in_specs=[VMEM, ANY, ANY] + [ANY] * len(after),
        out_specs=VMEM,
        out_shape=struct((rows, width), dtype),
        scratch_shapes=[
            pltpu.VMEM(w_in.shape, w_in.dtype),
            pltpu.VMEM(w_out.shape, w_out.dtype),
            pltpu.VMEM((rows, width), jnp.float32),
            pltpu.SemaphoreType.DMA((chunks,)),
            pltpu.SemaphoreType.DMA((chunks,)),
        ],
        compiler_params=params(52),
        cost_estimate=cost(1, 1),
    )(feats, w_in, w_out, *after)


def embed(feats, w_in, w_out, after):
    if lax.axis_size("tensor") == 1:
        return tower(feats, w_in, w_out, jnp.bfloat16, after)
    feats = lax.all_gather(feats, "tensor", axis=0, tiled=True)
    partial = tower(feats, w_in, w_out, jnp.float32, after)
    return lax.psum_scatter(partial, "tensor", scatter_dimension=0, tiled=True).astype(jnp.bfloat16)


def teacher_body(cols, planes, me, cands, count, owner, teacher, *refs):
    outs, dense, sems = refs[:cols], refs[cols], refs[cols + 1]
    rows = teacher.shape[0]
    slots = cands.shape[1]
    live = count[0]
    logits = teacher[...]
    usable = lax.broadcasted_iota(jnp.int32, logits.shape, 1) < live * rows
    shifted = logits - jnp.max(jnp.where(usable, logits, -jnp.inf), axis=1, keepdims=True)
    norm = jnp.sum(jnp.where(usable, jnp.exp(shifted), 0.0), axis=1, keepdims=True)
    log_p = shifted - jnp.log(norm)
    dense[...] = jnp.full(dense.shape, DEAD, jnp.float32)
    for k in range(slots):

        @pl.when(k < live)
        def _():
            apart = owner[cands[0, k]] ^ me[0]
            inside = apart % (CORES * cols)
            place = (inside % CORES) * planes + apart // (CORES * cols)
            dense[inside // CORES, place] = log_p[:, k * rows : (k + 1) * rows].T

    copies = [pltpu.make_async_copy(dense.at[i], outs[i], sems.at[i]) for i in range(cols)]
    for copy in copies:
        copy.start()
    for copy in copies:
        copy.wait()


def spread_teacher(cols, planes, me, cands, count, owner, teacher):
    rows = teacher.shape[0]
    places = CORES * planes
    return pl.pallas_call(
        functools.partial(teacher_body, cols, planes),
        in_specs=[SMEM, SMEM, SMEM, SMEM, VMEM],
        out_specs=[ANY] * cols,
        out_shape=[struct((places, rows, rows), jnp.float32)] * cols,
        scratch_shapes=[
            pltpu.VMEM((cols, places, rows, rows), jnp.float32),
            pltpu.SemaphoreType.DMA((cols,)),
        ],
        compiler_params=params(24),
        cost_estimate=cost(teacher.size, 8 * teacher.size),
    )(me, cands, count, owner, teacher)


def loads_of(sources, target, sems):
    rows = sources[0].shape[0]
    return [
        pltpu.make_async_copy(source, target.at[pl.ds(i * rows, rows)], sems.at[i]) for i, source in enumerate(sources)
    ]


def score_body(cols, places, scale, *refs):
    users, items, logs = refs[:cols], refs[cols : cols + places], refs[cols + places : 2 * cols + places]
    weights, stats, all_users, all_items, all_logs, user_sems, item_sems, log_sems = refs[2 * cols + places :]
    rows = users[0].shape[0]
    load_users = loads_of(users, all_users, user_sems)
    load_items = loads_of(items, all_items, item_sems)
    load_logs = loads_of(logs, all_logs, log_sems)
    for copy in load_items + load_users + load_logs:
        copy.start()
    for copy in load_items:
        copy.wait()
    step = 2 if cols % 2 == 0 else 1
    for first in range(0, cols, step):
        for i in range(first, first + step):
            load_users[i].wait()
        both = scale * lax.dot_general(
            all_items[...],
            all_users[first * rows : (first + step) * rows],
            (((1,), (1,)), ((), ())),
            preferred_element_type=jnp.float32,
        )
        for j in range(step):
            i = first + j
            load_logs[i].wait()
            score = both[:, j * rows : (j + 1) * rows]
            log_p = all_logs[i * places : (i + 1) * places].reshape(places * rows, rows)
            live = log_p > LIVE
            top = jnp.max(jnp.where(live, score, DEAD), axis=0, keepdims=True)
            shifted = score - top
            weight = jnp.where(live, jnp.exp(shifted), 0.0)
            prob = jnp.exp(log_p)
            weights[:, i * rows : (i + 1) * rows] = weight
            stats[0, i : i + 1, :] = top
            stats[1, i : i + 1, :] = jnp.sum(weight, axis=0, keepdims=True)
            stats[2, i : i + 1, :] = jnp.sum(jnp.where(live, prob * (log_p - shifted), 0.0), axis=0, keepdims=True)
            stats[3, i : i + 1, :] = jnp.sum(prob, axis=0, keepdims=True)


def scores(scale, users, items, logs):
    cols, places = len(users), len(items)
    rows, width = users[0].shape
    return pl.pallas_call(
        functools.partial(score_body, cols, places, scale),
        in_specs=[ANY] * (2 * cols + places),
        out_specs=[VMEM, VMEM],
        out_shape=[
            struct((places * rows, cols * rows), jnp.float32),
            struct((4, cols, rows), jnp.float32),
        ],
        scratch_shapes=[
            pltpu.VMEM((cols * rows, width), jnp.bfloat16),
            pltpu.VMEM((places * rows, width), jnp.bfloat16),
            pltpu.VMEM((cols * places, rows, rows), jnp.float32),
            pltpu.SemaphoreType.DMA((cols,)),
            pltpu.SemaphoreType.DMA((places,)),
            pltpu.SemaphoreType.DMA((cols,)),
        ],
        compiler_params=params(32),
        cost_estimate=cost(2 * cols * places * rows * rows * width, 8 * cols * places * rows * rows),
    )(*users, *items, *logs)


def far_body(cols, places, factor, *refs):
    stats, users, logs = refs[:cols], refs[cols : 2 * cols], refs[2 * cols : 3 * cols]
    weights, grads, divergence, far = refs[3 * cols : 3 * cols + 4]
    all_users, all_logs, user_sems, log_sems = refs[3 * cols + 4 :]
    rows = users[0].shape[0]
    load_users = loads_of(users, all_users, user_sems)
    load_logs = loads_of(logs, all_logs, log_sems)
    for copy in load_logs + load_users:
        copy.start()
    for i in range(cols):
        tops = [stats[j][0, i ^ j : (i ^ j) + 1, :] for j in range(cols)]
        sums = [stats[j][1, i ^ j : (i ^ j) + 1, :] for j in range(cols)]
        top = functools.reduce(jnp.maximum, tops)
        norm = functools.reduce(jnp.add, [s * jnp.exp(t - top) for s, t in zip(sums, tops)])
        ratio = jnp.exp(tops[0] - top) / norm
        if i == 0:
            lse = top + jnp.log(norm)
            terms = [stats[j][2, j : j + 1, :] + stats[j][3, j : j + 1, :] * (lse - tops[j]) for j in range(cols)]
            divergence[...] = functools.reduce(jnp.add, terms)
        load_logs[i].wait()
        prob = jnp.exp(all_logs[i * places : (i + 1) * places].reshape(places * rows, rows))
        lanes = slice(i * rows, (i + 1) * rows)
        grads[:, lanes] = (factor * (weights[:, lanes] * ratio - prob)).astype(jnp.bfloat16)
    for copy in load_users:
        copy.wait()
    half = places * rows // CORES
    far[...] = jnp.dot(grads[half:], all_users[...], preferred_element_type=jnp.float32).astype(far.dtype)


def far_parts(factor, stats, users, logs, weights):
    cols, places = len(users), logs[0].shape[0]
    rows, width = users[0].shape
    return pl.pallas_call(
        functools.partial(far_body, cols, places, factor),
        in_specs=[VMEM] * cols + [ANY] * (2 * cols) + [VMEM],
        out_specs=[VMEM] * 3,
        out_shape=[
            struct(weights.shape, jnp.bfloat16),
            struct((1, rows), jnp.float32),
            struct((places * rows // CORES, width), jnp.bfloat16),
        ],
        scratch_shapes=[
            pltpu.VMEM((cols * rows, width), jnp.bfloat16),
            pltpu.VMEM((cols * places, rows, rows), jnp.float32),
            pltpu.SemaphoreType.DMA((cols,)),
            pltpu.SemaphoreType.DMA((cols,)),
        ],
        compiler_params=params(32),
        cost_estimate=cost(cols * places * rows * rows * width, 8 * cols * places * rows * rows),
    )(*stats, *users, *logs, weights)


def near_body(cols, grads, *refs):
    users, (near, all_users, sems) = refs[:cols], refs[cols:]
    loads = loads_of(users, all_users, sems)
    for copy in loads:
        copy.start()
    for copy in loads:
        copy.wait()
    near[...] = jnp.dot(grads[: near.shape[0]], all_users[...], preferred_element_type=jnp.float32)


def near_part(grads, users):
    cols, places = len(users), grads.shape[0]
    rows, width = users[0].shape
    return pl.pallas_call(
        functools.partial(near_body, cols),
        in_specs=[VMEM] + [ANY] * cols,
        out_specs=VMEM,
        out_shape=struct((places // CORES, width), jnp.float32),
        scratch_shapes=[pltpu.VMEM((cols * rows, width), jnp.bfloat16), pltpu.SemaphoreType.DMA((cols,))],
        compiler_params=params(32),
        cost_estimate=cost(grads.size * width, 4 * grads.size),
    )(grads, *users)


def user_body(cols, places, grads, *refs):
    items, refs = refs[:places], refs[-cols - 2 :]
    parts, (all_items, sems) = refs[:cols], refs[cols:]
    rows = items[0].shape[0]
    loads = loads_of(items, all_items, sems)
    for copy in loads:
        copy.start()
    for copy in loads:
        copy.wait()
    for i in range(cols - 1, -1, -1):
        part = lax.dot_general(
            grads[:, i * rows : (i + 1) * rows],
            all_items[...],
            (((0,), (0,)), ((), ())),
            preferred_element_type=jnp.float32,
        )
        parts[i][...] = part.astype(parts[i].dtype)


def user_parts(cols, grads, items, after):
    places = len(items)
    rows, width = items[0].shape
    return pl.pallas_call(
        functools.partial(user_body, cols, places),
        in_specs=[VMEM] + [ANY] * (places + len(after)),
        out_specs=[VMEM] * cols,
        out_shape=[struct((rows, width), jnp.bfloat16 if i else jnp.float32) for i in range(cols)],
        scratch_shapes=[pltpu.VMEM((places * rows, width), jnp.bfloat16), pltpu.SemaphoreType.DMA((places,))],
        compiler_params=params(32),
        cost_estimate=cost(2 * grads.size * width, 4 * grads.size),
    )(grads, *items, *after)


def join_body(planes, near, far, *outs):
    rows = outs[0].shape[0]
    for i in range(planes - 1, -1, -1):
        part = slice(i * rows, (i + 1) * rows)
        outs[i][...] = (near[part] + far[part].astype(jnp.float32)).astype(outs[i].dtype)


def join(planes, near, far):
    rows, width = near.shape[0] // planes, near.shape[1]
    return pl.pallas_call(
        functools.partial(join_body, planes),
        in_specs=[VMEM, VMEM],
        out_specs=[VMEM] * planes,
        out_shape=[struct((rows, width), jnp.bfloat16 if i % 2 else jnp.float32) for i in range(planes)],
        compiler_params=params(24),
        cost_estimate=cost(near.size, 8 * near.size),
    )(near, far)


def shards(
    user_feats, item_feats, user_w_in, user_w_out, item_w_in, item_w_out, teacher, cand_blocks, cand_count, owner_map
):
    rows, width = user_feats.shape
    slots = cand_blocks.shape[1]
    count = lax.axis_size("dp")
    cols = 1 << ((count // CORES).bit_length() - 1) // 2
    planes = count // (CORES * cols)
    assert cols * planes * CORES == count and count & (count - 1) == 0
    scale = 3.0 / math.sqrt(width)
    factor = rows * slots / 4.0 * scale
    me = lax.axis_index("dp").reshape(1).astype(jnp.int32)

    def swap(array, apart):
        return lax.ppermute(array, "dp", [(i, i ^ apart) for i in range(count)])

    def over_columns(own):
        return [swap(own, c * CORES) for c in range(1, cols)]

    logs = spread_teacher(cols, planes, me, cand_blocks, cand_count, owner_map, teacher)
    first, *rest = logs
    logs = [first] + [swap(part, (c + 1) * CORES) for c, part in enumerate(rest)]

    item_emb = embed(item_feats, item_w_in, item_w_out, [first])
    wide = planes // 2
    crossed = [swap(item_emb, z * cols * CORES) for z in range(wide, planes if planes > 1 else 0, max(wide, 1))]
    nearby = [swap(item_emb, z * cols * CORES) for z in range(1, wide)]
    user_emb = embed(user_feats, user_w_in, user_w_out, [item_emb])
    user_emb, item_emb, logs, crossed, nearby = lax.optimization_barrier((user_emb, item_emb, logs, crossed, nearby))
    users = [user_emb] + over_columns(user_emb)
    derived = [swap(block, z * cols * CORES) for block in crossed for z in range(1, wide)]
    if cols > 1:
        users[1], item_emb, nearby, crossed = lax.optimization_barrier((users[1], item_emb, nearby, crossed))
    items = [item_emb] + nearby + crossed + derived
    items = items + [swap(block, 1) for block in items]

    weights, stats = scores(scale, users, items, logs)
    grads, divergence, far = far_parts(factor, [stats] + over_columns(stats), users, logs, weights)
    far = swap(far, 1)
    parts = join(planes, near_part(grads, users), far)
    hop = cols * CORES
    if planes == 4:
        merged = (parts[2] + swap(parts[3], hop).astype(jnp.float32)).astype(jnp.bfloat16)
        sent = [swap(merged, 2 * hop), swap(parts[1], hop)]
    else:
        sent = [swap(parts[z].astype(jnp.bfloat16), z * hop) for z in range(planes - 1, 0, -1)]
    own, *others = user_parts(cols, grads, items, [parts[0]])
    arrived = [swap(part, (c + 1) * CORES) for c, part in enumerate(others)]

    def add(start, parts):
        return functools.reduce(jnp.add, [part.astype(jnp.float32) for part in parts], start)

    return (divergence.reshape(rows), add(own, arrived), add(parts[0], sent))


def solution(mesh):
    both = ("dp", "tensor")
    placed = (
        P(both, None),
        P(both, None),
        P(None, "tensor"),
        P("tensor", None),
        P(None, "tensor"),
        P("tensor", None),
        P(both, None),
        P(both, None),
        P(both),
        P(),
    )
    return jax.shard_map(
        shards,
        mesh=mesh,
        in_specs=placed,
        out_specs=(P(both), P(both, None), P(both, None)),
        check_vma=False,
    )
```

```python
import functools
import math

import jax
import jax.numpy as jnp
from jax import lax
from jax.experimental import pallas as pl
from jax.experimental.pallas import tpu as pltpu
from jax.sharding import PartitionSpec as P

CORES = 2
LOWEST = -1e30
DEAD = -1.0
MIB = 1 << 20
ANY = pl.BlockSpec(memory_space=pl.ANY)
VMEM = pl.BlockSpec(memory_space=pltpu.VMEM)
SMEM = pl.BlockSpec(memory_space=pltpu.SMEM)


def struct(shape, dtype):
    return jax.ShapeDtypeStruct(shape, dtype)


def params(mib):
    return pltpu.CompilerParams(vmem_limit_bytes=mib * MIB)


def cost(flops, moved):
    return pl.CostEstimate(flops=int(flops), bytes_accessed=int(moved), transcendentals=0)


def tower_body(chunks, feats, w_in, w_out, *refs):
    out, held_in, held_out, total, sem_in, sem_out = refs[-6:]
    step = w_in.shape[1] // chunks

    def copies(i):
        part = pl.ds(pl.multiple_of(i * step, step), step)
        return (
            pltpu.make_async_copy(w_in.at[:, part], held_in.at[:, part], sem_in.at[i]),
            pltpu.make_async_copy(w_out.at[part], held_out.at[part], sem_out.at[i]),
        )

    for i in range(chunks):
        for copy in copies(i):
            copy.start()
    total[...] = jnp.zeros_like(total)

    def one(i, carry):
        first, second = copies(i)
        part = pl.ds(pl.multiple_of(i * step, step), step)
        first.wait()
        hidden = jnp.dot(feats[...], held_in[:, part], preferred_element_type=jnp.float32)
        hidden = jnp.maximum(hidden, 0.0).astype(jnp.bfloat16)
        second.wait()
        total[...] += jnp.dot(hidden, held_out[part], preferred_element_type=jnp.float32)
        return carry

    lax.fori_loop(0, chunks, one, 0)
    out[...] = total[...].astype(out.dtype)


def tower(feats, w_in, w_out, dtype, after):
    rows, width = feats.shape
    hidden = w_in.shape[1]
    chunks = max(1, hidden // 512)
    return pl.pallas_call(
        functools.partial(tower_body, chunks),
        in_specs=[VMEM, ANY, ANY] + [ANY] * len(after),
        out_specs=VMEM,
        out_shape=struct((rows, width), dtype),
        scratch_shapes=[
            pltpu.VMEM(w_in.shape, w_in.dtype),
            pltpu.VMEM(w_out.shape, w_out.dtype),
            pltpu.VMEM((rows, width), jnp.float32),
            pltpu.SemaphoreType.DMA((chunks,)),
            pltpu.SemaphoreType.DMA((chunks,)),
        ],
        compiler_params=params(52),
        cost_estimate=cost(1, 1),
    )(feats, w_in, w_out, *after)


def embed(feats, w_in, w_out, after):
    if lax.axis_size("tensor") == 1:
        return tower(feats, w_in, w_out, jnp.bfloat16, after)
    feats = lax.all_gather(feats, "tensor", axis=0, tiled=True)
    partial = tower(feats, w_in, w_out, jnp.float32, after)
    return lax.psum_scatter(partial, "tensor", scatter_dimension=0, tiled=True).astype(jnp.bfloat16)


def teacher_body(cols, planes, me, cands, count, owner, teacher, *refs):
    outs, (entropy, dense, sems) = refs[:cols], refs[cols:]
    rows = teacher.shape[0]
    slots = cands.shape[1]
    live = count[0]
    logits = teacher[...]
    usable = lax.broadcasted_iota(jnp.int32, logits.shape, 1) < live * rows
    shifted = logits - jnp.max(jnp.where(usable, logits, -jnp.inf), axis=1, keepdims=True)
    weight = jnp.where(usable, jnp.exp(shifted), 0.0)
    norm = jnp.sum(weight, axis=1, keepdims=True)
    prob = weight / norm
    log_sum = jnp.sum(jnp.where(usable, prob * (shifted - jnp.log(norm)), 0.0), axis=1, keepdims=True)
    entropy[...] = jnp.broadcast_to(log_sum, (rows, rows)).T[:1]
    dense[...] = jnp.full(dense.shape, DEAD, jnp.float32)
    for k in range(slots):

        @pl.when(k < live)
        def _():
            apart = owner[cands[0, k]] ^ me[0]
            inside = apart % (CORES * cols)
            place = (inside % CORES) * planes + apart // (CORES * cols)
            dense[inside // CORES, place] = prob[:, k * rows : (k + 1) * rows].T

    copies = [pltpu.make_async_copy(dense.at[i], outs[i], sems.at[i]) for i in range(cols)]
    for copy in copies:
        copy.start()
    for copy in copies:
        copy.wait()


def spread_teacher(cols, planes, me, cands, count, owner, teacher):
    rows = teacher.shape[0]
    places = CORES * planes
    return pl.pallas_call(
        functools.partial(teacher_body, cols, planes),
        in_specs=[SMEM, SMEM, SMEM, SMEM, VMEM],
        out_specs=[ANY] * cols + [VMEM],
        out_shape=[struct((places, rows, rows), jnp.float32)] * cols + [struct((1, rows), jnp.float32)],
        scratch_shapes=[
            pltpu.VMEM((cols, places, rows, rows), jnp.float32),
            pltpu.SemaphoreType.DMA((cols,)),
        ],
        compiler_params=params(24),
        cost_estimate=cost(teacher.size, 8 * teacher.size),
    )(me, cands, count, owner, teacher)


def lay(sources, target):
    rows = sources[0].shape[0]
    for i, source in enumerate(sources):
        target[i * rows : (i + 1) * rows] = source[...]


def score_body(cols, places, scale, *refs):
    users, items, probs = refs[:cols], refs[cols : cols + places], refs[cols + places : 2 * cols + places]
    weights, stats, all_users, all_items = refs[2 * cols + places :]
    rows = users[0].shape[0]
    lay(users, all_users)
    step = 2 if places % 2 == 0 else 1
    for first in range(0, places, step):
        lay(items[first : first + step], all_items)
        weights[first * rows : (first + step) * rows] = scale * lax.dot_general(
            all_items[: step * rows], all_users[...], (((1,), (1,)), ((), ())), preferred_element_type=jnp.float32
        )
    for i in range(cols):
        lanes = slice(i * rows, (i + 1) * rows)
        score = weights[:, lanes]
        prob = probs[i][...].reshape(places * rows, rows)
        live = prob >= 0.0
        prob = jnp.maximum(prob, 0.0)
        top = jnp.max(jnp.where(live, score, LOWEST), axis=0, keepdims=True)
        shifted = jnp.where(live, score - top, 0.0)
        weight = jnp.where(live, jnp.exp(shifted), 0.0)
        weights[:, lanes] = weight
        stats[0, i : i + 1, :] = top
        stats[1, i : i + 1, :] = jnp.sum(weight, axis=0, keepdims=True)
        stats[2, i : i + 1, :] = jnp.sum(prob * shifted, axis=0, keepdims=True)
        stats[3, i : i + 1, :] = jnp.sum(prob, axis=0, keepdims=True)


def scores(scale, users, items, probs):
    cols, places = len(users), len(items)
    rows, width = users[0].shape
    return pl.pallas_call(
        functools.partial(score_body, cols, places, scale),
        in_specs=[VMEM] * (2 * cols + places),
        out_specs=[VMEM, VMEM],
        out_shape=[
            struct((places * rows, cols * rows), jnp.float32),
            struct((4, cols, rows), jnp.float32),
        ],
        scratch_shapes=[pltpu.VMEM((cols * rows, width), jnp.bfloat16), pltpu.VMEM((2 * rows, width), jnp.bfloat16)],
        compiler_params=params(32),
        cost_estimate=cost(2 * cols * places * rows * rows * width, 8 * cols * places * rows * rows),
    )(*users, *items, *probs)


def far_body(cols, places, factor, entropy, *refs):
    stats, users, probs = refs[:cols], refs[cols : 2 * cols], refs[2 * cols : 3 * cols]
    weights, grads, divergence, far = refs[3 * cols : 3 * cols + 4]
    all_users = refs[3 * cols + 4]
    rows = users[0].shape[0]
    lay(users, all_users)
    for i in range(cols):
        tops = [stats[j][0, i ^ j : (i ^ j) + 1, :] for j in range(cols)]
        sums = [stats[j][1, i ^ j : (i ^ j) + 1, :] for j in range(cols)]
        top = functools.reduce(jnp.maximum, tops)
        norm = functools.reduce(jnp.add, [s * jnp.exp(t - top) for s, t in zip(sums, tops)])
        ratio = jnp.exp(tops[0] - top) / norm
        if i == 0:
            lse = top + jnp.log(norm)
            terms = [stats[j][3, j : j + 1, :] * (lse - tops[j]) - stats[j][2, j : j + 1, :] for j in range(cols)]
            divergence[...] = functools.reduce(jnp.add, terms, entropy[...])
        prob = jnp.maximum(probs[i][...].reshape(places * rows, rows), 0.0)
        lanes = slice(i * rows, (i + 1) * rows)
        grads[:, lanes] = (factor * (weights[:, lanes] * ratio - prob)).astype(jnp.bfloat16)
    half = places * rows // CORES
    far[...] = jnp.dot(grads[half:], all_users[...], preferred_element_type=jnp.float32).astype(far.dtype)


def far_parts(factor, entropy, stats, users, probs, weights):
    cols, places = len(users), probs[0].shape[0]
    rows, width = users[0].shape
    return pl.pallas_call(
        functools.partial(far_body, cols, places, factor),
        in_specs=[VMEM] * (2 + 3 * cols),
        out_specs=[VMEM] * 3,
        out_shape=[
            struct(weights.shape, jnp.bfloat16),
            struct((1, rows), jnp.float32),
            struct((places * rows // CORES, width), jnp.bfloat16),
        ],
        scratch_shapes=[pltpu.VMEM((cols * rows, width), jnp.bfloat16)],
        compiler_params=params(32),
        cost_estimate=cost(cols * places * rows * rows * width, 8 * cols * places * rows * rows),
    )(entropy, *stats, *users, *probs, weights)


def near_body(cols, grads, *refs):
    users, (near, all_users) = refs[:cols], refs[cols:]
    lay(users, all_users)
    near[...] = jnp.dot(grads[: near.shape[0]], all_users[...], preferred_element_type=jnp.float32)


def near_part(grads, users):
    cols, places = len(users), grads.shape[0]
    rows, width = users[0].shape
    return pl.pallas_call(
        functools.partial(near_body, cols),
        in_specs=[VMEM] * (1 + cols),
        out_specs=VMEM,
        out_shape=struct((places // CORES, width), jnp.float32),
        scratch_shapes=[pltpu.VMEM((cols * rows, width), jnp.bfloat16)],
        compiler_params=params(32),
        cost_estimate=cost(grads.size * width, 4 * grads.size),
    )(grads, *users)


def user_body(cols, places, grads, *refs):
    items, refs = refs[:places], refs[-cols - 1 :]
    parts, all_items = refs[:cols], refs[cols]
    rows = items[0].shape[0]
    lay(items, all_items)
    for i in range(cols - 1, -1, -1):
        part = lax.dot_general(
            grads[:, i * rows : (i + 1) * rows],
            all_items[...],
            (((0,), (0,)), ((), ())),
            preferred_element_type=jnp.float32,
        )
        parts[i][...] = part.astype(parts[i].dtype)


def user_parts(cols, grads, items, after):
    places = len(items)
    rows, width = items[0].shape
    return pl.pallas_call(
        functools.partial(user_body, cols, places),
        in_specs=[VMEM] * (1 + places) + [ANY] * len(after),
        out_specs=[VMEM] * cols,
        out_shape=[struct((rows, width), jnp.bfloat16 if i else jnp.float32) for i in range(cols)],
        scratch_shapes=[pltpu.VMEM((places * rows, width), jnp.bfloat16)],
        compiler_params=params(32),
        cost_estimate=cost(2 * grads.size * width, 4 * grads.size),
    )(grads, *items, *after)


def join_body(planes, near, far, *outs):
    rows = outs[0].shape[0]
    for i in range(planes - 1, -1, -1):
        part = slice(i * rows, (i + 1) * rows)
        outs[i][...] = (near[part] + far[part].astype(jnp.float32)).astype(outs[i].dtype)


def join(planes, near, far):
    rows, width = near.shape[0] // planes, near.shape[1]
    return pl.pallas_call(
        functools.partial(join_body, planes),
        in_specs=[VMEM, VMEM],
        out_specs=[VMEM] * planes,
        out_shape=[struct((rows, width), jnp.bfloat16 if i % 2 else jnp.float32) for i in range(planes)],
        compiler_params=params(24),
        cost_estimate=cost(near.size, 8 * near.size),
    )(near, far)


def shards(
    user_feats, item_feats, user_w_in, user_w_out, item_w_in, item_w_out, teacher, cand_blocks, cand_count, owner_map
):
    rows, width = user_feats.shape
    slots = cand_blocks.shape[1]
    count = lax.axis_size("dp")
    cols = 1 << ((count // CORES).bit_length() - 1) // 2
    planes = count // (CORES * cols)
    assert cols * planes * CORES == count and count & (count - 1) == 0
    scale = 3.0 / math.sqrt(width)
    factor = rows * slots / 4.0 * scale
    me = lax.axis_index("dp").reshape(1).astype(jnp.int32)

    def swap(array, apart):
        return lax.ppermute(array, "dp", [(i, i ^ apart) for i in range(count)])

    def over_columns(own):
        return [swap(own, c * CORES) for c in range(1, cols)]

    *probs, entropy = spread_teacher(cols, planes, me, cand_blocks, cand_count, owner_map, teacher)
    first, *rest = probs
    probs = [first] + [swap(part, (c + 1) * CORES) for c, part in enumerate(rest)]

    item_emb = embed(item_feats, item_w_in, item_w_out, [first])
    wide = planes // 2
    crossed = [swap(item_emb, z * cols * CORES) for z in range(wide, planes if planes > 1 else 0, max(wide, 1))]
    nearby = [swap(item_emb, z * cols * CORES) for z in range(1, wide)]
    user_emb = embed(user_feats, user_w_in, user_w_out, [item_emb])
    user_emb, item_emb, probs, crossed, nearby = lax.optimization_barrier((user_emb, item_emb, probs, crossed, nearby))
    users = [user_emb] + over_columns(user_emb)
    derived = [swap(block, z * cols * CORES) for block in crossed for z in range(1, wide)]
    if cols > 1:
        users[1], item_emb, nearby, crossed = lax.optimization_barrier((users[1], item_emb, nearby, crossed))
    items = [item_emb] + nearby + crossed + derived
    items = items + [swap(block, 1) for block in items]

    weights, stats = scores(scale, users, items, probs)
    grads, divergence, far = far_parts(factor, entropy, [stats] + over_columns(stats), users, probs, weights)
    far = swap(far, 1)
    parts = join(planes, near_part(grads, users), far)
    hop = cols * CORES
    if planes == 4:
        merged = (parts[2] + swap(parts[3], hop).astype(jnp.float32)).astype(jnp.bfloat16)
        sent = [swap(merged, 2 * hop), swap(parts[1], hop)]
    else:
        sent = [swap(parts[z].astype(jnp.bfloat16), z * hop) for z in range(planes - 1, 0, -1)]
    own, *others = user_parts(cols, grads, items, [parts[0]])
    arrived = [swap(part, (c + 1) * CORES) for c, part in enumerate(others)]

    def add(start, parts):
        return functools.reduce(jnp.add, [part.astype(jnp.float32) for part in parts], start)

    return (divergence.reshape(rows), add(own, arrived), add(parts[0], sent))


def solution(mesh):
    both = ("dp", "tensor")
    placed = (
        P(both, None),
        P(both, None),
        P(None, "tensor"),
        P("tensor", None),
        P(None, "tensor"),
        P("tensor", None),
        P(both, None),
        P(both, None),
        P(both),
        P(),
    )
    return jax.shard_map(
        shards,
        mesh=mesh,
        in_specs=placed,
        out_specs=(P(both), P(both, None), P(both, None)),
        check_vma=False,
    )
```

```python
import functools
import math

import jax
import jax.numpy as jnp
from jax import lax
from jax.experimental import pallas as pl
from jax.experimental.pallas import tpu as pltpu
from jax.sharding import PartitionSpec as P

CORES = 2
LOWEST = -1e30
DEAD = -1.0
MIB = 1 << 20
ANY = pl.BlockSpec(memory_space=pl.ANY)
VMEM = pl.BlockSpec(memory_space=pltpu.VMEM)
SMEM = pl.BlockSpec(memory_space=pltpu.SMEM)


def struct(shape, dtype):
    return jax.ShapeDtypeStruct(shape, dtype)


def params(mib):
    return pltpu.CompilerParams(vmem_limit_bytes=mib * MIB)


def cost(flops, moved):
    return pl.CostEstimate(flops=int(flops), bytes_accessed=int(moved), transcendentals=0)


def in_hbm(array):
    return pltpu.with_memory_space_constraint(array, pltpu.HBM)


def tower_body(chunks, held, feats, w_in, w_out, *refs):
    out, held_in, held_out, total, sem_in, sem_out, *own = refs[-6 if held else -8 :]
    if not held:
        load = pltpu.make_async_copy(feats, *own)
        load.start()
        load.wait()
        feats = own[0]
    step = w_in.shape[1] // chunks

    def copies(i):
        part = pl.ds(pl.multiple_of(i * step, step), step)
        return (
            pltpu.make_async_copy(w_in.at[:, part], held_in.at[:, part], sem_in.at[i]),
            pltpu.make_async_copy(w_out.at[part], held_out.at[part], sem_out.at[i]),
        )

    for i in range(chunks):
        for copy in copies(i):
            copy.start()
    total[...] = jnp.zeros_like(total)

    def one(i, carry):
        first, second = copies(i)
        part = pl.ds(pl.multiple_of(i * step, step), step)
        first.wait()
        hidden = jnp.dot(feats[...], held_in[:, part], preferred_element_type=jnp.float32)
        hidden = jnp.maximum(hidden, 0.0).astype(jnp.bfloat16)
        second.wait()
        total[...] += jnp.dot(hidden, held_out[part], preferred_element_type=jnp.float32)
        return carry

    lax.fori_loop(0, chunks, one, 0)
    out[...] = total[...].astype(out.dtype)


def tower(feats, w_in, w_out, dtype, after, held):
    rows, width = feats.shape
    hidden = w_in.shape[1]
    chunks = max(1, hidden // 512)
    return pl.pallas_call(
        functools.partial(tower_body, chunks, held),
        in_specs=[VMEM if held else ANY, ANY, ANY] + [ANY] * len(after),
        out_specs=VMEM,
        out_shape=struct((rows, width), dtype),
        scratch_shapes=[
            pltpu.VMEM(w_in.shape, w_in.dtype),
            pltpu.VMEM(w_out.shape, w_out.dtype),
            pltpu.VMEM((rows, width), jnp.float32),
            pltpu.SemaphoreType.DMA((chunks,)),
            pltpu.SemaphoreType.DMA((chunks,)),
        ]
        + ([] if held else [pltpu.VMEM(feats.shape, feats.dtype), pltpu.SemaphoreType.DMA]),
        compiler_params=params(52),
        cost_estimate=cost(1, 1),
    )(feats if held else in_hbm(feats), w_in, w_out, *after)


def embed(feats, w_in, w_out, after, held):
    if lax.axis_size("tensor") == 1:
        return tower(feats, w_in, w_out, jnp.bfloat16, after, held)
    feats = lax.all_gather(feats, "tensor", axis=0, tiled=True)
    partial = tower(feats, w_in, w_out, jnp.float32, after, held)
    return lax.psum_scatter(partial, "tensor", scatter_dimension=0, tiled=True).astype(jnp.bfloat16)


def teacher_body(cols, planes, me, cands_hbm, count, owner_hbm, teacher_hbm, *refs):
    outs, (entropy, dense, sems, teacher, cands, owner, load_sems) = refs[:cols], refs[cols:]
    loads = [
        pltpu.make_async_copy(source, target, load_sems.at[i])
        for i, (source, target) in enumerate([(teacher_hbm, teacher), (cands_hbm, cands), (owner_hbm, owner)])
    ]
    for copy in loads:
        copy.start()
    dense[...] = jnp.full(dense.shape, DEAD, jnp.float32)
    for copy in loads:
        copy.wait()
    rows = teacher.shape[0]
    slots = cands.shape[1]
    live = count[0]
    logits = teacher[...]
    usable = lax.broadcasted_iota(jnp.int32, logits.shape, 1) < live * rows
    shifted = logits - jnp.max(jnp.where(usable, logits, -jnp.inf), axis=1, keepdims=True)
    weight = jnp.where(usable, jnp.exp(shifted), 0.0)
    norm = jnp.sum(weight, axis=1, keepdims=True)
    prob = weight / norm
    log_sum = jnp.sum(jnp.where(usable, prob * (shifted - jnp.log(norm)), 0.0), axis=1, keepdims=True)
    entropy[...] = jnp.broadcast_to(log_sum, (rows, rows)).T[:1]
    for k in range(slots):

        @pl.when(k < live)
        def _():
            apart = owner[cands[0, k]] ^ me[0]
            inside = apart % (CORES * cols)
            place = (inside % CORES) * planes + apart // (CORES * cols)
            dense[inside // CORES, place] = prob[:, k * rows : (k + 1) * rows].T

    copies = [pltpu.make_async_copy(dense.at[i], outs[i], sems.at[i]) for i in range(cols)]
    for copy in copies:
        copy.start()
    for copy in copies:
        copy.wait()


def spread_teacher(cols, planes, me, cands, count, owner, teacher):
    rows = teacher.shape[0]
    places = CORES * planes
    return pl.pallas_call(
        functools.partial(teacher_body, cols, planes),
        in_specs=[SMEM, ANY, SMEM, ANY, ANY],
        out_specs=[ANY] * cols + [VMEM],
        out_shape=[struct((places, rows, rows), jnp.float32)] * cols + [struct((1, rows), jnp.float32)],
        scratch_shapes=[
            pltpu.VMEM((cols, places, rows, rows), jnp.float32),
            pltpu.SemaphoreType.DMA((cols,)),
            pltpu.VMEM(teacher.shape, teacher.dtype),
            pltpu.SMEM(cands.shape, cands.dtype),
            pltpu.SMEM(owner.shape, owner.dtype),
            pltpu.SemaphoreType.DMA((3,)),
        ],
        compiler_params=params(24),
        cost_estimate=cost(teacher.size, 8 * teacher.size),
    )(me, in_hbm(cands), count, in_hbm(owner), in_hbm(teacher))


def lay(sources, target):
    rows = sources[0].shape[0]
    for i, source in enumerate(sources):
        target[i * rows : (i + 1) * rows] = source[...]


def score_body(cols, places, scale, *refs):
    users, items, probs = refs[:cols], refs[cols : cols + places], refs[cols + places : 2 * cols + places]
    weights, stats, all_users, all_items = refs[2 * cols + places :]
    rows = users[0].shape[0]
    lay(users, all_users)
    step = 2 if places % 2 == 0 else 1
    for first in range(0, places, step):
        lay(items[first : first + step], all_items)
        weights[first * rows : (first + step) * rows] = scale * lax.dot_general(
            all_items[: step * rows], all_users[...], (((1,), (1,)), ((), ())), preferred_element_type=jnp.float32
        )
    for i in range(cols):
        lanes = slice(i * rows, (i + 1) * rows)
        score = weights[:, lanes]
        prob = probs[i][...].reshape(places * rows, rows)
        live = prob >= 0.0
        prob = jnp.maximum(prob, 0.0)
        top = jnp.max(jnp.where(live, score, LOWEST), axis=0, keepdims=True)
        shifted = jnp.where(live, score - top, 0.0)
        weight = jnp.where(live, jnp.exp(shifted), 0.0)
        weights[:, lanes] = weight
        stats[0, i : i + 1, :] = top
        stats[1, i : i + 1, :] = jnp.sum(weight, axis=0, keepdims=True)
        stats[2, i : i + 1, :] = jnp.sum(prob * shifted, axis=0, keepdims=True)
        stats[3, i : i + 1, :] = jnp.sum(prob, axis=0, keepdims=True)


def scores(scale, users, items, probs):
    cols, places = len(users), len(items)
    rows, width = users[0].shape
    return pl.pallas_call(
        functools.partial(score_body, cols, places, scale),
        in_specs=[VMEM] * (2 * cols + places),
        out_specs=[VMEM, VMEM],
        out_shape=[
            struct((places * rows, cols * rows), jnp.float32),
            struct((4, cols, rows), jnp.float32),
        ],
        scratch_shapes=[pltpu.VMEM((cols * rows, width), jnp.bfloat16), pltpu.VMEM((2 * rows, width), jnp.bfloat16)],
        compiler_params=params(32),
        cost_estimate=cost(2 * cols * places * rows * rows * width, 8 * cols * places * rows * rows),
    )(*users, *items, *probs)


def far_body(cols, places, factor, entropy, *refs):
    stats, users, probs = refs[:cols], refs[cols : 2 * cols], refs[2 * cols : 3 * cols]
    weights, grads, divergence, far = refs[3 * cols : 3 * cols + 4]
    all_users = refs[3 * cols + 4]
    rows = users[0].shape[0]
    lay(users, all_users)
    for i in range(cols):
        tops = [stats[j][0, i ^ j : (i ^ j) + 1, :] for j in range(cols)]
        sums = [stats[j][1, i ^ j : (i ^ j) + 1, :] for j in range(cols)]
        top = functools.reduce(jnp.maximum, tops)
        norm = functools.reduce(jnp.add, [s * jnp.exp(t - top) for s, t in zip(sums, tops)])
        ratio = jnp.exp(tops[0] - top) / norm
        if i == 0:
            lse = top + jnp.log(norm)
            terms = [stats[j][3, j : j + 1, :] * (lse - tops[j]) - stats[j][2, j : j + 1, :] for j in range(cols)]
            divergence[...] = functools.reduce(jnp.add, terms, entropy[...])
        prob = jnp.maximum(probs[i][...].reshape(places * rows, rows), 0.0)
        lanes = slice(i * rows, (i + 1) * rows)
        grads[:, lanes] = (factor * (weights[:, lanes] * ratio - prob)).astype(jnp.bfloat16)
    half = places * rows // CORES
    far[...] = jnp.dot(grads[half:], all_users[...], preferred_element_type=jnp.float32).astype(far.dtype)


def far_parts(factor, entropy, stats, users, probs, weights):
    cols, places = len(users), probs[0].shape[0]
    rows, width = users[0].shape
    return pl.pallas_call(
        functools.partial(far_body, cols, places, factor),
        in_specs=[VMEM] * (2 + 3 * cols),
        out_specs=[VMEM] * 3,
        out_shape=[
            struct(weights.shape, jnp.bfloat16),
            struct((1, rows), jnp.float32),
            struct((places * rows // CORES, width), jnp.bfloat16),
        ],
        scratch_shapes=[pltpu.VMEM((cols * rows, width), jnp.bfloat16)],
        compiler_params=params(32),
        cost_estimate=cost(cols * places * rows * rows * width, 8 * cols * places * rows * rows),
    )(entropy, *stats, *users, *probs, weights)


def near_body(cols, grads, *refs):
    users, (near, all_users) = refs[:cols], refs[cols:]
    lay(users, all_users)
    near[...] = jnp.dot(grads[: near.shape[0]], all_users[...], preferred_element_type=jnp.float32)


def near_part(grads, users):
    cols, places = len(users), grads.shape[0]
    rows, width = users[0].shape
    return pl.pallas_call(
        functools.partial(near_body, cols),
        in_specs=[VMEM] * (1 + cols),
        out_specs=VMEM,
        out_shape=struct((places // CORES, width), jnp.float32),
        scratch_shapes=[pltpu.VMEM((cols * rows, width), jnp.bfloat16)],
        compiler_params=params(32),
        cost_estimate=cost(grads.size * width, 4 * grads.size),
    )(grads, *users)


def user_body(cols, places, grads, *refs):
    items, refs = refs[:places], refs[-cols - 1 :]
    parts, all_items = refs[:cols], refs[cols]
    rows = items[0].shape[0]
    lay(items, all_items)
    for i in range(cols - 1, -1, -1):
        part = lax.dot_general(
            grads[:, i * rows : (i + 1) * rows],
            all_items[...],
            (((0,), (0,)), ((), ())),
            preferred_element_type=jnp.float32,
        )
        parts[i][...] = part.astype(parts[i].dtype)


def user_parts(cols, grads, items, after):
    places = len(items)
    rows, width = items[0].shape
    return pl.pallas_call(
        functools.partial(user_body, cols, places),
        in_specs=[VMEM] * (1 + places) + [ANY] * len(after),
        out_specs=[VMEM] * cols,
        out_shape=[struct((rows, width), jnp.bfloat16 if i else jnp.float32) for i in range(cols)],
        scratch_shapes=[pltpu.VMEM((places * rows, width), jnp.bfloat16)],
        compiler_params=params(32),
        cost_estimate=cost(2 * grads.size * width, 4 * grads.size),
    )(grads, *items, *after)


def join_body(planes, near, far, *outs):
    rows = outs[0].shape[0]
    for i in range(planes - 1, -1, -1):
        part = slice(i * rows, (i + 1) * rows)
        outs[i][...] = (near[part] + far[part].astype(jnp.float32)).astype(outs[i].dtype)


def join(planes, near, far):
    rows, width = near.shape[0] // planes, near.shape[1]
    return pl.pallas_call(
        functools.partial(join_body, planes),
        in_specs=[VMEM, VMEM],
        out_specs=[VMEM] * planes,
        out_shape=[struct((rows, width), jnp.bfloat16 if i % 2 else jnp.float32) for i in range(planes)],
        compiler_params=params(24),
        cost_estimate=cost(near.size, 8 * near.size),
    )(near, far)


def shards(
    user_feats, item_feats, user_w_in, user_w_out, item_w_in, item_w_out, teacher, cand_blocks, cand_count, owner_map
):
    rows, width = user_feats.shape
    slots = cand_blocks.shape[1]
    count = lax.axis_size("dp")
    cols = 1 << ((count // CORES).bit_length() - 1) // 2
    planes = count // (CORES * cols)
    assert cols * planes * CORES == count and count & (count - 1) == 0
    scale = 3.0 / math.sqrt(width)
    factor = rows * slots / 4.0 * scale
    me = lax.axis_index("dp").reshape(1).astype(jnp.int32)

    def swap(array, apart):
        return lax.ppermute(array, "dp", [(i, i ^ apart) for i in range(count)])

    def over_columns(own):
        return [swap(own, c * CORES) for c in range(1, cols)]

    *probs, entropy = spread_teacher(cols, planes, me, cand_blocks, cand_count, owner_map, teacher)
    first, *rest = probs
    probs = [first] + [swap(part, (c + 1) * CORES) for c, part in enumerate(rest)]

    item_emb = embed(item_feats, item_w_in, item_w_out, [first], False)
    wide = planes // 2
    crossed = [swap(item_emb, z * cols * CORES) for z in range(wide, planes if planes > 1 else 0, max(wide, 1))]
    nearby = [swap(item_emb, z * cols * CORES) for z in range(1, wide)]
    user_emb = embed(user_feats, user_w_in, user_w_out, [item_emb], True)
    user_emb, item_emb, probs, crossed, nearby = lax.optimization_barrier((user_emb, item_emb, probs, crossed, nearby))
    users = [user_emb] + over_columns(user_emb)
    derived = [swap(block, z * cols * CORES) for block in crossed for z in range(1, wide)]
    if cols > 1:
        users[1], item_emb, nearby, crossed = lax.optimization_barrier((users[1], item_emb, nearby, crossed))
    items = [item_emb] + nearby + crossed + derived
    items = items + [swap(block, 1) for block in items]

    weights, stats = scores(scale, users, items, probs)
    grads, divergence, far = far_parts(factor, entropy, [stats] + over_columns(stats), users, probs, weights)
    far = swap(far, 1)
    parts = join(planes, near_part(grads, users), far)
    hop = cols * CORES
    if planes == 4:
        merged = (parts[2] + swap(parts[3], hop).astype(jnp.float32)).astype(jnp.bfloat16)
        sent = [swap(merged, 2 * hop), swap(parts[1], hop)]
    else:
        sent = [swap(parts[z].astype(jnp.bfloat16), z * hop) for z in range(planes - 1, 0, -1)]
    own, *others = user_parts(cols, grads, items, [parts[0]])
    arrived = [swap(part, (c + 1) * CORES) for c, part in enumerate(others)]

    def add(start, parts):
        return functools.reduce(jnp.add, [part.astype(jnp.float32) for part in parts], start)

    return (divergence.reshape(rows), add(own, arrived), add(parts[0], sent))


def solution(mesh):
    both = ("dp", "tensor")
    placed = (
        P(both, None),
        P(both, None),
        P(None, "tensor"),
        P("tensor", None),
        P(None, "tensor"),
        P("tensor", None),
        P(both, None),
        P(both, None),
        P(both),
        P(),
    )
    return jax.shard_map(
        shards,
        mesh=mesh,
        in_specs=placed,
        out_specs=(P(both), P(both, None), P(both, None)),
        check_vma=False,
    )
```

```python
import functools
import math

import jax
import jax.numpy as jnp
from jax import lax
from jax.experimental import pallas as pl
from jax.experimental.pallas import tpu as pltpu
from jax.sharding import PartitionSpec as P

CORES = 2
LOWEST = -1e30
DEAD = -1.0
MIB = 1 << 20
ANY = pl.BlockSpec(memory_space=pl.ANY)
VMEM = pl.BlockSpec(memory_space=pltpu.VMEM)
SMEM = pl.BlockSpec(memory_space=pltpu.SMEM)


def struct(shape, dtype):
    return jax.ShapeDtypeStruct(shape, dtype)


def params(mib):
    return pltpu.CompilerParams(vmem_limit_bytes=mib * MIB)


def cost(flops, moved):
    return pl.CostEstimate(flops=int(flops), bytes_accessed=int(moved), transcendentals=0)


def in_hbm(array):
    return pltpu.with_memory_space_constraint(array, pltpu.HBM)


def tower_body(chunks, held, feats, w_in, w_out, *refs):
    out, held_in, held_out, total, sem_in, sem_out, *own = refs[-6 if held else -8 :]
    step = w_in.shape[1] // chunks
    ahead = 0 if held else 1

    def copies(i):
        part = pl.ds(pl.multiple_of(i * step, step), step)
        return (
            pltpu.make_async_copy(w_in.at[:, part], held_in.at[:, part], sem_in.at[i]),
            pltpu.make_async_copy(w_out.at[part], held_out.at[part], sem_out.at[i]),
        )

    if not held:
        load = pltpu.make_async_copy(feats, *own)
        load.start()
        for copy in copies(0):
            copy.start()
        load.wait()
        feats = own[0]
    for i in range(ahead, chunks):
        for copy in copies(i):
            copy.start()
    total[...] = jnp.zeros_like(total)

    def one(i, carry):
        first, second = copies(i)
        part = pl.ds(pl.multiple_of(i * step, step), step)
        first.wait()
        hidden = jnp.dot(feats[...], held_in[:, part], preferred_element_type=jnp.float32)
        hidden = jnp.maximum(hidden, 0.0).astype(jnp.bfloat16)
        second.wait()
        total[...] += jnp.dot(hidden, held_out[part], preferred_element_type=jnp.float32)
        return carry

    lax.fori_loop(0, chunks, one, 0, unroll=True)
    out[...] = total[...].astype(out.dtype)


def tower(feats, w_in, w_out, dtype, after, held):
    rows, width = feats.shape
    hidden = w_in.shape[1]
    chunks = max(1, hidden // 512)
    return pl.pallas_call(
        functools.partial(tower_body, chunks, held),
        in_specs=[VMEM if held else ANY, ANY, ANY] + [ANY] * len(after),
        out_specs=VMEM,
        out_shape=struct((rows, width), dtype),
        scratch_shapes=[
            pltpu.VMEM(w_in.shape, w_in.dtype),
            pltpu.VMEM(w_out.shape, w_out.dtype),
            pltpu.VMEM((rows, width), jnp.float32),
            pltpu.SemaphoreType.DMA((chunks,)),
            pltpu.SemaphoreType.DMA((chunks,)),
        ]
        + ([] if held else [pltpu.VMEM(feats.shape, feats.dtype), pltpu.SemaphoreType.DMA]),
        compiler_params=params(52),
        cost_estimate=cost(1, 1),
    )(feats if held else in_hbm(feats), w_in, w_out, *after)


def embed(feats, w_in, w_out, after, held):
    if lax.axis_size("tensor") == 1:
        return tower(feats, w_in, w_out, jnp.bfloat16, after, held)
    feats = lax.all_gather(feats, "tensor", axis=0, tiled=True)
    partial = tower(feats, w_in, w_out, jnp.float32, after, held)
    return lax.psum_scatter(partial, "tensor", scatter_dimension=0, tiled=True).astype(jnp.bfloat16)


def teacher_body(cols, planes, me, cands_hbm, count, owner_hbm, teacher_hbm, *refs):
    outs, (entropy, dense, sems, teacher, cands, owner, load_sems) = refs[:cols], refs[cols:]
    loads = [
        pltpu.make_async_copy(source, target, load_sems.at[i])
        for i, (source, target) in enumerate([(teacher_hbm, teacher), (cands_hbm, cands), (owner_hbm, owner)])
    ]
    for copy in loads:
        copy.start()
    dense[...] = jnp.full(dense.shape, DEAD, jnp.float32)
    for copy in loads:
        copy.wait()
    rows = teacher.shape[0]
    slots = cands.shape[1]
    live = count[0]
    logits = teacher[...]
    usable = lax.broadcasted_iota(jnp.int32, logits.shape, 1) < live * rows
    shifted = logits - jnp.max(jnp.where(usable, logits, -jnp.inf), axis=1, keepdims=True)
    weight = jnp.where(usable, jnp.exp(shifted), 0.0)
    norm = jnp.sum(weight, axis=1, keepdims=True)
    prob = weight / norm
    log_sum = jnp.sum(jnp.where(usable, prob * (shifted - jnp.log(norm)), 0.0), axis=1, keepdims=True)
    entropy[...] = jnp.broadcast_to(log_sum, (rows, rows)).T[:1]
    for k in range(slots):

        @pl.when(k < live)
        def _():
            apart = owner[cands[0, k]] ^ me[0]
            inside = apart % (CORES * cols)
            place = (inside % CORES) * planes + apart // (CORES * cols)
            dense[inside // CORES, place] = prob[:, k * rows : (k + 1) * rows].T

    copies = [pltpu.make_async_copy(dense.at[i], outs[i], sems.at[i]) for i in range(cols)]
    for copy in copies:
        copy.start()
    for copy in copies:
        copy.wait()


def spread_teacher(cols, planes, me, cands, count, owner, teacher):
    rows = teacher.shape[0]
    places = CORES * planes
    return pl.pallas_call(
        functools.partial(teacher_body, cols, planes),
        in_specs=[SMEM, ANY, SMEM, ANY, ANY],
        out_specs=[ANY] * cols + [VMEM],
        out_shape=[struct((places, rows, rows), jnp.float32)] * cols + [struct((1, rows), jnp.float32)],
        scratch_shapes=[
            pltpu.VMEM((cols, places, rows, rows), jnp.float32),
            pltpu.SemaphoreType.DMA((cols,)),
            pltpu.VMEM(teacher.shape, teacher.dtype),
            pltpu.SMEM(cands.shape, cands.dtype),
            pltpu.SMEM(owner.shape, owner.dtype),
            pltpu.SemaphoreType.DMA((3,)),
        ],
        compiler_params=params(24),
        cost_estimate=cost(teacher.size, 8 * teacher.size),
    )(me, in_hbm(cands), count, in_hbm(owner), in_hbm(teacher))


def lay(sources, target):
    rows = sources[0].shape[0]
    for i, source in enumerate(sources):
        target[i * rows : (i + 1) * rows] = source[...]


def score_body(cols, places, scale, *refs):
    users, items, probs = refs[:cols], refs[cols : cols + places], refs[cols + places : 2 * cols + places]
    weights, stats, all_users, all_items = refs[2 * cols + places :]
    rows = users[0].shape[0]
    lay(users, all_users)
    step = 2 if places % 2 == 0 else 1
    for first in range(0, places, step):
        lay(items[first : first + step], all_items)
        weights[first * rows : (first + step) * rows] = scale * lax.dot_general(
            all_items[: step * rows], all_users[...], (((1,), (1,)), ((), ())), preferred_element_type=jnp.float32
        )
    for i in range(cols):
        lanes = slice(i * rows, (i + 1) * rows)
        score = weights[:, lanes]
        prob = probs[i][...].reshape(places * rows, rows)
        live = prob >= 0.0
        prob = jnp.maximum(prob, 0.0)
        top = jnp.max(jnp.where(live, score, LOWEST), axis=0, keepdims=True)
        shifted = jnp.where(live, score - top, 0.0)
        weight = jnp.where(live, jnp.exp(shifted), 0.0)
        weights[:, lanes] = weight
        stats[0, i : i + 1, :] = top
        stats[1, i : i + 1, :] = jnp.sum(weight, axis=0, keepdims=True)
        stats[2, i : i + 1, :] = jnp.sum(prob * shifted, axis=0, keepdims=True)
        stats[3, i : i + 1, :] = jnp.sum(prob, axis=0, keepdims=True)


def scores(scale, users, items, probs):
    cols, places = len(users), len(items)
    rows, width = users[0].shape
    return pl.pallas_call(
        functools.partial(score_body, cols, places, scale),
        in_specs=[VMEM] * (2 * cols + places),
        out_specs=[VMEM, VMEM],
        out_shape=[
            struct((places * rows, cols * rows), jnp.float32),
            struct((4, cols, rows), jnp.float32),
        ],
        scratch_shapes=[pltpu.VMEM((cols * rows, width), jnp.bfloat16), pltpu.VMEM((2 * rows, width), jnp.bfloat16)],
        compiler_params=params(32),
        cost_estimate=cost(2 * cols * places * rows * rows * width, 8 * cols * places * rows * rows),
    )(*users, *items, *probs)


def far_body(cols, places, factor, entropy, *refs):
    stats, users, probs = refs[:cols], refs[cols : 2 * cols], refs[2 * cols : 3 * cols]
    weights, grads, divergence, far = refs[3 * cols : 3 * cols + 4]
    all_users = refs[3 * cols + 4]
    rows = users[0].shape[0]
    lay(users, all_users)
    for i in range(cols):
        tops = [stats[j][0, i ^ j : (i ^ j) + 1, :] for j in range(cols)]
        sums = [stats[j][1, i ^ j : (i ^ j) + 1, :] for j in range(cols)]
        top = functools.reduce(jnp.maximum, tops)
        norm = functools.reduce(jnp.add, [s * jnp.exp(t - top) for s, t in zip(sums, tops)])
        ratio = jnp.exp(tops[0] - top) / norm
        if i == 0:
            lse = top + jnp.log(norm)
            terms = [stats[j][3, j : j + 1, :] * (lse - tops[j]) - stats[j][2, j : j + 1, :] for j in range(cols)]
            divergence[...] = functools.reduce(jnp.add, terms, entropy[...])
        prob = jnp.maximum(probs[i][...].reshape(places * rows, rows), 0.0)
        lanes = slice(i * rows, (i + 1) * rows)
        grads[:, lanes] = (factor * (weights[:, lanes] * ratio - prob)).astype(jnp.bfloat16)
    half = places * rows // CORES
    far[...] = jnp.dot(grads[half:], all_users[...], preferred_element_type=jnp.float32).astype(far.dtype)


def far_parts(factor, entropy, stats, users, probs, weights):
    cols, places = len(users), probs[0].shape[0]
    rows, width = users[0].shape
    return pl.pallas_call(
        functools.partial(far_body, cols, places, factor),
        in_specs=[VMEM] * (2 + 3 * cols),
        out_specs=[VMEM] * 3,
        out_shape=[
            struct(weights.shape, jnp.bfloat16),
            struct((1, rows), jnp.float32),
            struct((places * rows // CORES, width), jnp.bfloat16),
        ],
        scratch_shapes=[pltpu.VMEM((cols * rows, width), jnp.bfloat16)],
        compiler_params=params(32),
        cost_estimate=cost(cols * places * rows * rows * width, 8 * cols * places * rows * rows),
    )(entropy, *stats, *users, *probs, weights)


def near_body(cols, grads, *refs):
    users, (near, all_users) = refs[:cols], refs[cols:]
    lay(users, all_users)
    near[...] = jnp.dot(grads[: near.shape[0]], all_users[...], preferred_element_type=jnp.float32)


def near_part(grads, users):
    cols, places = len(users), grads.shape[0]
    rows, width = users[0].shape
    return pl.pallas_call(
        functools.partial(near_body, cols),
        in_specs=[VMEM] * (1 + cols),
        out_specs=VMEM,
        out_shape=struct((places // CORES, width), jnp.float32),
        scratch_shapes=[pltpu.VMEM((cols * rows, width), jnp.bfloat16)],
        compiler_params=params(32),
        cost_estimate=cost(grads.size * width, 4 * grads.size),
    )(grads, *users)


def user_body(cols, places, grads, *refs):
    items, refs = refs[:places], refs[-cols - 1 :]
    parts, all_items = refs[:cols], refs[cols]
    rows = items[0].shape[0]
    lay(items, all_items)
    for i in range(cols - 1, -1, -1):
        part = lax.dot_general(
            grads[:, i * rows : (i + 1) * rows],
            all_items[...],
            (((0,), (0,)), ((), ())),
            preferred_element_type=jnp.float32,
        )
        parts[i][...] = part.astype(parts[i].dtype)


def user_parts(cols, grads, items, after):
    places = len(items)
    rows, width = items[0].shape
    return pl.pallas_call(
        functools.partial(user_body, cols, places),
        in_specs=[VMEM] * (1 + places) + [ANY] * len(after),
        out_specs=[VMEM] * cols,
        out_shape=[struct((rows, width), jnp.bfloat16 if i else jnp.float32) for i in range(cols)],
        scratch_shapes=[pltpu.VMEM((places * rows, width), jnp.bfloat16)],
        compiler_params=params(32),
        cost_estimate=cost(2 * grads.size * width, 4 * grads.size),
    )(grads, *items, *after)


def join_body(planes, near, far, *outs):
    rows = outs[0].shape[0]
    for i in range(planes - 1, -1, -1):
        part = slice(i * rows, (i + 1) * rows)
        outs[i][...] = (near[part] + far[part].astype(jnp.float32)).astype(outs[i].dtype)


def join(planes, near, far):
    rows, width = near.shape[0] // planes, near.shape[1]
    return pl.pallas_call(
        functools.partial(join_body, planes),
        in_specs=[VMEM, VMEM],
        out_specs=[VMEM] * planes,
        out_shape=[struct((rows, width), jnp.bfloat16 if i % 2 else jnp.float32) for i in range(planes)],
        compiler_params=params(24),
        cost_estimate=cost(near.size, 8 * near.size),
    )(near, far)


def shards(
    user_feats, item_feats, user_w_in, user_w_out, item_w_in, item_w_out, teacher, cand_blocks, cand_count, owner_map
):
    rows, width = user_feats.shape
    slots = cand_blocks.shape[1]
    count = lax.axis_size("dp")
    cols = 1 << ((count // CORES).bit_length() - 1) // 2
    planes = count // (CORES * cols)
    assert cols * planes * CORES == count and count & (count - 1) == 0
    scale = 3.0 / math.sqrt(width)
    factor = rows * slots / 4.0 * scale
    me = lax.axis_index("dp").reshape(1).astype(jnp.int32)

    def swap(array, apart):
        return lax.ppermute(array, "dp", [(i, i ^ apart) for i in range(count)])

    def over_columns(own):
        return [swap(own, c * CORES) for c in range(1, cols)]

    *probs, entropy = spread_teacher(cols, planes, me, cand_blocks, cand_count, owner_map, teacher)
    first, *rest = probs
    probs = [first] + [swap(part, (c + 1) * CORES) for c, part in enumerate(rest)]

    item_emb = embed(item_feats, item_w_in, item_w_out, [first], False)
    wide = planes // 2
    crossed = [swap(item_emb, z * cols * CORES) for z in range(wide, planes if planes > 1 else 0, max(wide, 1))]
    nearby = [swap(item_emb, z * cols * CORES) for z in range(1, wide)]
    user_emb = embed(user_feats, user_w_in, user_w_out, [item_emb], True)
    user_emb, item_emb, probs, crossed, nearby = lax.optimization_barrier((user_emb, item_emb, probs, crossed, nearby))
    users = [user_emb] + over_columns(user_emb)
    derived = [swap(block, z * cols * CORES) for block in crossed for z in range(1, wide)]
    if cols > 1:
        users[1], item_emb, nearby, crossed = lax.optimization_barrier((users[1], item_emb, nearby, crossed))
    items = [item_emb] + nearby + crossed + derived
    items = items + [swap(block, 1) for block in items]

    weights, stats = scores(scale, users, items, probs)
    grads, divergence, far = far_parts(factor, entropy, [stats] + over_columns(stats), users, probs, weights)
    far = swap(far, 1)
    parts = join(planes, near_part(grads, users), far)
    hop = cols * CORES
    if planes == 4:
        merged = (parts[2] + swap(parts[3], hop).astype(jnp.float32)).astype(jnp.bfloat16)
        sent = [swap(merged, 2 * hop), swap(parts[1], hop)]
    else:
        sent = [swap(parts[z].astype(jnp.bfloat16), z * hop) for z in range(planes - 1, 0, -1)]
    own, *others = user_parts(cols, grads, items, [parts[0]])
    arrived = [swap(part, (c + 1) * CORES) for c, part in enumerate(others)]

    def add(start, parts):
        return functools.reduce(jnp.add, [part.astype(jnp.float32) for part in parts], start)

    return (divergence.reshape(rows), add(own, arrived), add(parts[0], sent))


def solution(mesh):
    both = ("dp", "tensor")
    placed = (
        P(both, None),
        P(both, None),
        P(None, "tensor"),
        P("tensor", None),
        P(None, "tensor"),
        P("tensor", None),
        P(both, None),
        P(both, None),
        P(both),
        P(),
    )
    return jax.shard_map(
        shards,
        mesh=mesh,
        in_specs=placed,
        out_specs=(P(both), P(both, None), P(both, None)),
        check_vma=False,
    )
```

```python
import functools
import math

import jax
import jax.numpy as jnp
from jax import lax
from jax.experimental import pallas as pl
from jax.experimental.pallas import tpu as pltpu
from jax.sharding import PartitionSpec as P

CORES = 2
LOWEST = -1e30
DEAD = -1.0
MIB = 1 << 20
ANY = pl.BlockSpec(memory_space=pl.ANY)
VMEM = pl.BlockSpec(memory_space=pltpu.VMEM)
SMEM = pl.BlockSpec(memory_space=pltpu.SMEM)


def struct(shape, dtype):
    return jax.ShapeDtypeStruct(shape, dtype)


def params(mib):
    return pltpu.CompilerParams(vmem_limit_bytes=mib * MIB)


def cost(flops, moved):
    return pl.CostEstimate(flops=int(flops), bytes_accessed=int(moved), transcendentals=0)


def in_hbm(array):
    return pltpu.with_memory_space_constraint(array, pltpu.HBM)


def tower_body(chunks, ready, feats, w_in, w_out, *refs):
    out, held_out, total, sem_out, *own = refs[-4 if ready else -6 :]
    step = w_in.shape[1] // chunks

    def part(i):
        return pl.ds(pl.multiple_of(i * step, step), step)

    def copies(i):
        both = [pltpu.make_async_copy(w_out.at[part(i)], held_out.at[part(i)], sem_out.at[i])]
        if not ready:
            both.insert(0, pltpu.make_async_copy(w_in.at[:, part(i)], own[0].at[:, part(i)], own[1].at[i]))
        return both

    for i in range(chunks):
        for copy in copies(i):
            copy.start()
    total[...] = jnp.zeros_like(total)
    held_in = w_in if ready else own[0]

    def one(i, carry):
        waits = copies(i)
        if not ready:
            waits[0].wait()
        hidden = jnp.dot(feats[...], held_in[:, part(i)], preferred_element_type=jnp.float32)
        hidden = jnp.maximum(hidden, 0.0).astype(jnp.bfloat16)
        waits[-1].wait()
        total[...] += jnp.dot(hidden, held_out[part(i)], preferred_element_type=jnp.float32)
        return carry

    lax.fori_loop(0, chunks, one, 0, unroll=True)
    out[...] = total[...].astype(out.dtype)


def tower(feats, w_in, w_out, dtype, after, ready):
    rows, width = feats.shape
    hidden = w_in.shape[1]
    chunks = max(1, hidden // 512)
    own = [] if ready else [pltpu.VMEM(w_in.shape, w_in.dtype), pltpu.SemaphoreType.DMA((chunks,))]
    return pl.pallas_call(
        functools.partial(tower_body, chunks, ready),
        in_specs=[VMEM, VMEM if ready else ANY, ANY] + [ANY] * len(after),
        out_specs=VMEM,
        out_shape=struct((rows, width), dtype),
        scratch_shapes=[
            pltpu.VMEM(w_out.shape, w_out.dtype),
            pltpu.VMEM((rows, width), jnp.float32),
            pltpu.SemaphoreType.DMA((chunks,)),
        ]
        + own,
        compiler_params=params(20 if ready else 52),
        cost_estimate=cost(1, 1),
    )(feats, w_in if ready else in_hbm(w_in), in_hbm(w_out), *after)


def embed(feats, w_in, w_out, after, ready):
    if lax.axis_size("tensor") == 1:
        return tower(feats, w_in, w_out, jnp.bfloat16, after, ready)
    feats = lax.all_gather(feats, "tensor", axis=0, tiled=True)
    partial = tower(feats, w_in, w_out, jnp.float32, after, ready)
    return lax.psum_scatter(partial, "tensor", scatter_dimension=0, tiled=True).astype(jnp.bfloat16)


def teacher_body(cols, planes, me, cands_hbm, count, owner_hbm, teacher_hbm, *refs):
    outs, (entropy, dense, sems, teacher, cands, owner, load_sems) = refs[:cols], refs[cols:]
    loads = [
        pltpu.make_async_copy(source, target, load_sems.at[i])
        for i, (source, target) in enumerate([(teacher_hbm, teacher), (cands_hbm, cands), (owner_hbm, owner)])
    ]
    for copy in loads:
        copy.start()
    dense[...] = jnp.full(dense.shape, DEAD, jnp.float32)
    for copy in loads:
        copy.wait()
    rows = teacher.shape[0]
    slots = cands.shape[1]
    live = count[0]
    logits = teacher[...]
    usable = lax.broadcasted_iota(jnp.int32, logits.shape, 1) < live * rows
    shifted = logits - jnp.max(jnp.where(usable, logits, -jnp.inf), axis=1, keepdims=True)
    weight = jnp.where(usable, jnp.exp(shifted), 0.0)
    norm = jnp.sum(weight, axis=1, keepdims=True)
    prob = weight / norm
    log_sum = jnp.sum(jnp.where(usable, prob * (shifted - jnp.log(norm)), 0.0), axis=1, keepdims=True)
    entropy[...] = jnp.broadcast_to(log_sum, (rows, rows)).T[:1]
    for k in range(slots):

        @pl.when(k < live)
        def _():
            apart = owner[cands[0, k]] ^ me[0]
            inside = apart % (CORES * cols)
            place = (inside % CORES) * planes + apart // (CORES * cols)
            dense[inside // CORES, place] = prob[:, k * rows : (k + 1) * rows].T

    copies = [pltpu.make_async_copy(dense.at[i], outs[i], sems.at[i]) for i in range(cols)]
    for copy in copies:
        copy.start()
    for copy in copies:
        copy.wait()


def spread_teacher(cols, planes, me, cands, count, owner, teacher):
    rows = teacher.shape[0]
    places = CORES * planes
    return pl.pallas_call(
        functools.partial(teacher_body, cols, planes),
        in_specs=[SMEM, ANY, SMEM, ANY, ANY],
        out_specs=[ANY] * cols + [VMEM],
        out_shape=[struct((places, rows, rows), jnp.float32)] * cols + [struct((1, rows), jnp.float32)],
        scratch_shapes=[
            pltpu.VMEM((cols, places, rows, rows), jnp.float32),
            pltpu.SemaphoreType.DMA((cols,)),
            pltpu.VMEM(teacher.shape, teacher.dtype),
            pltpu.SMEM(cands.shape, cands.dtype),
            pltpu.SMEM(owner.shape, owner.dtype),
            pltpu.SemaphoreType.DMA((3,)),
        ],
        compiler_params=params(24),
        cost_estimate=cost(10**10, 8 * teacher.size),
    )(me, in_hbm(cands), count, in_hbm(owner), in_hbm(teacher))


def lay(sources, target):
    rows = sources[0].shape[0]
    for i, source in enumerate(sources):
        target[i * rows : (i + 1) * rows] = source[...]


def score_body(cols, places, scale, *refs):
    users, items, probs = refs[:cols], refs[cols : cols + places], refs[cols + places : 2 * cols + places]
    weights, stats, all_users, all_items = refs[2 * cols + places :]
    rows = users[0].shape[0]
    lay(users, all_users)
    step = 2 if places % 2 == 0 else 1
    for first in range(0, places, step):
        lay(items[first : first + step], all_items)
        weights[first * rows : (first + step) * rows] = scale * lax.dot_general(
            all_items[: step * rows], all_users[...], (((1,), (1,)), ((), ())), preferred_element_type=jnp.float32
        )
    for i in range(cols):
        lanes = slice(i * rows, (i + 1) * rows)
        score = weights[:, lanes]
        prob = probs[i][...].reshape(places * rows, rows)
        live = prob >= 0.0
        prob = jnp.maximum(prob, 0.0)
        top = jnp.max(jnp.where(live, score, LOWEST), axis=0, keepdims=True)
        shifted = jnp.where(live, score - top, 0.0)
        weight = jnp.where(live, jnp.exp(shifted), 0.0)
        weights[:, lanes] = weight
        stats[0, i : i + 1, :] = top
        stats[1, i : i + 1, :] = jnp.sum(weight, axis=0, keepdims=True)
        stats[2, i : i + 1, :] = jnp.sum(prob * shifted, axis=0, keepdims=True)
        stats[3, i : i + 1, :] = jnp.sum(prob, axis=0, keepdims=True)


def scores(scale, users, items, probs):
    cols, places = len(users), len(items)
    rows, width = users[0].shape
    return pl.pallas_call(
        functools.partial(score_body, cols, places, scale),
        in_specs=[VMEM] * (2 * cols + places),
        out_specs=[VMEM, VMEM],
        out_shape=[
            struct((places * rows, cols * rows), jnp.float32),
            struct((4, cols, rows), jnp.float32),
        ],
        scratch_shapes=[pltpu.VMEM((cols * rows, width), jnp.bfloat16), pltpu.VMEM((2 * rows, width), jnp.bfloat16)],
        compiler_params=params(32),
        cost_estimate=cost(2 * cols * places * rows * rows * width, 8 * cols * places * rows * rows),
    )(*users, *items, *probs)


def far_body(cols, places, factor, entropy, *refs):
    stats, users, probs = refs[:cols], refs[cols : 2 * cols], refs[2 * cols : 3 * cols]
    weights, grads, divergence, far = refs[3 * cols : 3 * cols + 4]
    all_users = refs[3 * cols + 4]
    rows = users[0].shape[0]
    lay(users, all_users)
    for i in range(cols):
        tops = [stats[j][0, i ^ j : (i ^ j) + 1, :] for j in range(cols)]
        sums = [stats[j][1, i ^ j : (i ^ j) + 1, :] for j in range(cols)]
        top = functools.reduce(jnp.maximum, tops)
        norm = functools.reduce(jnp.add, [s * jnp.exp(t - top) for s, t in zip(sums, tops)])
        ratio = jnp.exp(tops[0] - top) / norm
        if i == 0:
            lse = top + jnp.log(norm)
            terms = [stats[j][3, j : j + 1, :] * (lse - tops[j]) - stats[j][2, j : j + 1, :] for j in range(cols)]
            divergence[...] = functools.reduce(jnp.add, terms, entropy[...])
        prob = jnp.maximum(probs[i][...].reshape(places * rows, rows), 0.0)
        lanes = slice(i * rows, (i + 1) * rows)
        grads[:, lanes] = (factor * (weights[:, lanes] * ratio - prob)).astype(jnp.bfloat16)
    half = places * rows // CORES
    far[...] = jnp.dot(grads[half:], all_users[...], preferred_element_type=jnp.float32).astype(far.dtype)


def far_parts(factor, entropy, stats, users, probs, weights):
    cols, places = len(users), probs[0].shape[0]
    rows, width = users[0].shape
    return pl.pallas_call(
        functools.partial(far_body, cols, places, factor),
        in_specs=[VMEM] * (2 + 3 * cols),
        out_specs=[VMEM] * 3,
        out_shape=[
            struct(weights.shape, jnp.bfloat16),
            struct((1, rows), jnp.float32),
            struct((places * rows // CORES, width), jnp.bfloat16),
        ],
        scratch_shapes=[pltpu.VMEM((cols * rows, width), jnp.bfloat16)],
        compiler_params=params(32),
        cost_estimate=cost(cols * places * rows * rows * width, 8 * cols * places * rows * rows),
    )(entropy, *stats, *users, *probs, weights)


def near_body(cols, grads, *refs):
    users, (near, all_users) = refs[:cols], refs[cols:]
    lay(users, all_users)
    near[...] = jnp.dot(grads[: near.shape[0]], all_users[...], preferred_element_type=jnp.float32)


def near_part(grads, users):
    cols, places = len(users), grads.shape[0]
    rows, width = users[0].shape
    return pl.pallas_call(
        functools.partial(near_body, cols),
        in_specs=[VMEM] * (1 + cols),
        out_specs=VMEM,
        out_shape=struct((places // CORES, width), jnp.float32),
        scratch_shapes=[pltpu.VMEM((cols * rows, width), jnp.bfloat16)],
        compiler_params=params(32),
        cost_estimate=cost(grads.size * width, 4 * grads.size),
    )(grads, *users)


def user_body(cols, places, grads, *refs):
    items, refs = refs[:places], refs[-cols - 1 :]
    parts, all_items = refs[:cols], refs[cols]
    rows = items[0].shape[0]
    lay(items, all_items)
    for i in range(cols - 1, -1, -1):
        part = lax.dot_general(
            grads[:, i * rows : (i + 1) * rows],
            all_items[...],
            (((0,), (0,)), ((), ())),
            preferred_element_type=jnp.float32,
        )
        parts[i][...] = part.astype(parts[i].dtype)


def user_parts(cols, grads, items, after):
    places = len(items)
    rows, width = items[0].shape
    return pl.pallas_call(
        functools.partial(user_body, cols, places),
        in_specs=[VMEM] * (1 + places) + [ANY] * len(after),
        out_specs=[VMEM] * cols,
        out_shape=[struct((rows, width), jnp.bfloat16 if i else jnp.float32) for i in range(cols)],
        scratch_shapes=[pltpu.VMEM((places * rows, width), jnp.bfloat16)],
        compiler_params=params(32),
        cost_estimate=cost(2 * grads.size * width, 4 * grads.size),
    )(grads, *items, *after)


def join_body(planes, near, far, *outs):
    rows = outs[0].shape[0]
    for i in range(planes - 1, -1, -1):
        part = slice(i * rows, (i + 1) * rows)
        outs[i][...] = (near[part] + far[part].astype(jnp.float32)).astype(outs[i].dtype)


def join(planes, near, far):
    rows, width = near.shape[0] // planes, near.shape[1]
    return pl.pallas_call(
        functools.partial(join_body, planes),
        in_specs=[VMEM, VMEM],
        out_specs=[VMEM] * planes,
        out_shape=[struct((rows, width), jnp.bfloat16 if i % 2 else jnp.float32) for i in range(planes)],
        compiler_params=params(24),
        cost_estimate=cost(near.size, 8 * near.size),
    )(near, far)


def shards(
    user_feats, item_feats, user_w_in, user_w_out, item_w_in, item_w_out, teacher, cand_blocks, cand_count, owner_map
):
    rows, width = user_feats.shape
    slots = cand_blocks.shape[1]
    count = lax.axis_size("dp")
    cols = 1 << ((count // CORES).bit_length() - 1) // 2
    planes = count // (CORES * cols)
    assert cols * planes * CORES == count and count & (count - 1) == 0
    scale = 3.0 / math.sqrt(width)
    factor = rows * slots / 4.0 * scale
    me = lax.axis_index("dp").reshape(1).astype(jnp.int32)

    def swap(array, apart):
        return lax.ppermute(array, "dp", [(i, i ^ apart) for i in range(count)])

    def over_columns(own):
        return [swap(own, c * CORES) for c in range(1, cols)]

    *probs, entropy = spread_teacher(cols, planes, me, cand_blocks, cand_count, owner_map, teacher)
    first, *rest = probs
    probs = [first] + [swap(part, (c + 1) * CORES) for c, part in enumerate(rest)]

    item_emb = embed(item_feats, item_w_in, item_w_out, [first], True)
    wide = planes // 2
    crossed = [swap(item_emb, z * cols * CORES) for z in range(wide, planes if planes > 1 else 0, max(wide, 1))]
    nearby = [swap(item_emb, z * cols * CORES) for z in range(1, wide)]
    user_emb = embed(user_feats, user_w_in, user_w_out, [item_emb], False)
    user_emb, item_emb, probs, crossed, nearby = lax.optimization_barrier((user_emb, item_emb, probs, crossed, nearby))
    users = [user_emb] + over_columns(user_emb)
    derived = [swap(block, z * cols * CORES) for block in crossed for z in range(1, wide)]
    if cols > 1:
        users[1], item_emb, nearby, crossed = lax.optimization_barrier((users[1], item_emb, nearby, crossed))
    items = [item_emb] + nearby + crossed + derived
    items = items + [swap(block, 1) for block in items]

    weights, stats = scores(scale, users, items, probs)
    grads, divergence, far = far_parts(factor, entropy, [stats] + over_columns(stats), users, probs, weights)
    far = swap(far, 1)
    parts = join(planes, near_part(grads, users), far)
    hop = cols * CORES
    if planes == 4:
        merged = (parts[2] + swap(parts[3], hop).astype(jnp.float32)).astype(jnp.bfloat16)
        sent = [swap(merged, 2 * hop), swap(parts[1], hop)]
    else:
        sent = [swap(parts[z].astype(jnp.bfloat16), z * hop) for z in range(planes - 1, 0, -1)]
    own, *others = user_parts(cols, grads, items, [parts[0]])
    arrived = [swap(part, (c + 1) * CORES) for c, part in enumerate(others)]

    def add(start, parts):
        return functools.reduce(jnp.add, [part.astype(jnp.float32) for part in parts], start)

    return (divergence.reshape(rows), add(own, arrived), add(parts[0], sent))


def solution(mesh):
    both = ("dp", "tensor")
    placed = (
        P(both, None),
        P(both, None),
        P(None, "tensor"),
        P("tensor", None),
        P(None, "tensor"),
        P("tensor", None),
        P(both, None),
        P(both, None),
        P(both),
        P(),
    )
    return jax.shard_map(
        shards,
        mesh=mesh,
        in_specs=placed,
        out_specs=(P(both), P(both, None), P(both, None)),
        check_vma=False,
    )
```

```python
import functools
import math

import jax
import jax.numpy as jnp
from jax import lax
from jax.experimental import pallas as pl
from jax.experimental.pallas import tpu as pltpu
from jax.sharding import PartitionSpec as P

CORES = 2
LOWEST = -1e30
DEAD = -1.0
MIB = 1 << 20
ANY = pl.BlockSpec(memory_space=pl.ANY)
VMEM = pl.BlockSpec(memory_space=pltpu.VMEM)
SMEM = pl.BlockSpec(memory_space=pltpu.SMEM)


def struct(shape, dtype):
    return jax.ShapeDtypeStruct(shape, dtype)


def params(mib):
    return pltpu.CompilerParams(vmem_limit_bytes=mib * MIB)


def cost(flops, moved):
    return pl.CostEstimate(flops=int(flops), bytes_accessed=int(moved), transcendentals=0)


def in_hbm(array):
    return pltpu.with_memory_space_constraint(array, pltpu.HBM)


def tower_body(chunks, ready, feats, w_in, w_out, *refs):
    out, held_out, total, sem_out, *own = refs[-4 if ready else -6 :]
    step = w_in.shape[1] // chunks

    def part(i):
        return pl.ds(pl.multiple_of(i * step, step), step)

    def copies(i):
        both = [pltpu.make_async_copy(w_out.at[part(i)], held_out.at[part(i)], sem_out.at[i])]
        if not ready:
            both.insert(0, pltpu.make_async_copy(w_in.at[:, part(i)], own[0].at[:, part(i)], own[1].at[i]))
        return both

    for i in range(chunks):
        for copy in copies(i):
            copy.start()
    total[...] = jnp.zeros_like(total)
    held_in = w_in if ready else own[0]

    def one(i, carry):
        waits = copies(i)
        if not ready:
            waits[0].wait()
        hidden = jnp.dot(feats[...], held_in[:, part(i)], preferred_element_type=jnp.float32)
        hidden = jnp.maximum(hidden, 0.0).astype(jnp.bfloat16)
        waits[-1].wait()
        total[...] += jnp.dot(hidden, held_out[part(i)], preferred_element_type=jnp.float32)
        return carry

    lax.fori_loop(0, chunks, one, 0, unroll=True)
    out[...] = total[...].astype(out.dtype)


def tower(feats, w_in, w_out, dtype, after, ready):
    rows, width = feats.shape
    hidden = w_in.shape[1]
    chunks = max(1, hidden // (2048 if ready else 1024))
    own = [] if ready else [pltpu.VMEM(w_in.shape, w_in.dtype), pltpu.SemaphoreType.DMA((chunks,))]
    return pl.pallas_call(
        functools.partial(tower_body, chunks, ready),
        in_specs=[VMEM, VMEM if ready else ANY, ANY] + [ANY] * len(after),
        out_specs=VMEM,
        out_shape=struct((rows, width), dtype),
        scratch_shapes=[
            pltpu.VMEM(w_out.shape, w_out.dtype),
            pltpu.VMEM((rows, width), jnp.float32),
            pltpu.SemaphoreType.DMA((chunks,)),
        ]
        + own,
        compiler_params=params(20 if ready else 52),
        cost_estimate=cost(1, 1),
    )(feats, w_in if ready else in_hbm(w_in), in_hbm(w_out), *after)


def embed(feats, w_in, w_out, after, ready):
    if lax.axis_size("tensor") == 1:
        return tower(feats, w_in, w_out, jnp.bfloat16, after, ready)
    feats = lax.all_gather(feats, "tensor", axis=0, tiled=True)
    partial = tower(feats, w_in, w_out, jnp.float32, after, ready)
    return lax.psum_scatter(partial, "tensor", scatter_dimension=0, tiled=True).astype(jnp.bfloat16)


def teacher_body(cols, planes, me, cands_hbm, count, owner_hbm, teacher_hbm, *refs):
    outs, (entropy, dense, sems, teacher, cands, owner, load_sems) = refs[:cols], refs[cols:]
    loads = [
        pltpu.make_async_copy(source, target, load_sems.at[i])
        for i, (source, target) in enumerate([(teacher_hbm, teacher), (cands_hbm, cands), (owner_hbm, owner)])
    ]
    for copy in loads:
        copy.start()
    dense[...] = jnp.full(dense.shape, DEAD, jnp.float32)
    for copy in loads:
        copy.wait()
    rows = teacher.shape[0]
    slots = cands.shape[1]
    live = count[0]
    logits = teacher[...]
    usable = lax.broadcasted_iota(jnp.int32, logits.shape, 1) < live * rows
    shifted = logits - jnp.max(jnp.where(usable, logits, -jnp.inf), axis=1, keepdims=True)
    weight = jnp.where(usable, jnp.exp(shifted), 0.0)
    norm = jnp.sum(weight, axis=1, keepdims=True)
    prob = weight / norm
    log_sum = jnp.sum(jnp.where(usable, prob * (shifted - jnp.log(norm)), 0.0), axis=1, keepdims=True)
    entropy[...] = jnp.broadcast_to(log_sum, (rows, rows)).T[:1]
    for k in range(slots):

        @pl.when(k < live)
        def _():
            apart = owner[cands[0, k]] ^ me[0]
            inside = apart % (CORES * cols)
            place = (inside % CORES) * planes + apart // (CORES * cols)
            dense[inside // CORES, place] = prob[:, k * rows : (k + 1) * rows]

    copies = [pltpu.make_async_copy(dense.at[i], outs[i], sems.at[i]) for i in range(cols)]
    for copy in copies:
        copy.start()
    for copy in copies:
        copy.wait()


def spread_teacher(cols, planes, me, cands, count, owner, teacher):
    rows = teacher.shape[0]
    places = CORES * planes
    return pl.pallas_call(
        functools.partial(teacher_body, cols, planes),
        in_specs=[SMEM, ANY, SMEM, ANY, ANY],
        out_specs=[ANY] * cols + [VMEM],
        out_shape=[struct((places, rows, rows), jnp.float32)] * cols + [struct((1, rows), jnp.float32)],
        scratch_shapes=[
            pltpu.VMEM((cols, places, rows, rows), jnp.float32),
            pltpu.SemaphoreType.DMA((cols,)),
            pltpu.VMEM(teacher.shape, teacher.dtype),
            pltpu.SMEM(cands.shape, cands.dtype),
            pltpu.SMEM(owner.shape, owner.dtype),
            pltpu.SemaphoreType.DMA((3,)),
        ],
        compiler_params=params(24),
        cost_estimate=cost(10**10, 8 * teacher.size),
    )(me, in_hbm(cands), count, in_hbm(owner), in_hbm(teacher))


def turn_body(cols, *refs):
    for source, out in zip(refs[:cols], refs[cols:]):
        for i in range(source.shape[0]):
            out[i] = source[i].T


def turned(probs):
    return pl.pallas_call(
        functools.partial(turn_body, len(probs)),
        in_specs=[VMEM] * len(probs),
        out_specs=[VMEM] * len(probs),
        out_shape=[struct(part.shape, part.dtype) for part in probs],
        compiler_params=params(24),
        cost_estimate=cost(1, 1),
    )(*probs)


def lay(sources, target):
    rows = sources[0].shape[0]
    for i, source in enumerate(sources):
        target[i * rows : (i + 1) * rows] = source[...]


def score_body(cols, places, scale, *refs):
    users, items, probs = refs[:cols], refs[cols : cols + places], refs[cols + places : 2 * cols + places]
    weights, stats, all_users, all_items = refs[2 * cols + places :]
    rows = users[0].shape[0]
    lay(users, all_users)
    step = 2 if places % 2 == 0 else 1
    for first in range(0, places, step):
        lay(items[first : first + step], all_items)
        weights[first * rows : (first + step) * rows] = scale * lax.dot_general(
            all_items[: step * rows], all_users[...], (((1,), (1,)), ((), ())), preferred_element_type=jnp.float32
        )
    for i in range(cols):
        lanes = slice(i * rows, (i + 1) * rows)
        score = weights[:, lanes]
        prob = probs[i][...].reshape(places * rows, rows)
        live = prob >= 0.0
        prob = jnp.maximum(prob, 0.0)
        top = jnp.max(jnp.where(live, score, LOWEST), axis=0, keepdims=True)
        shifted = jnp.where(live, score - top, 0.0)
        weight = jnp.where(live, jnp.exp(shifted), 0.0)
        weights[:, lanes] = weight
        stats[0, i : i + 1, :] = top
        stats[1, i : i + 1, :] = jnp.sum(weight, axis=0, keepdims=True)
        stats[2, i : i + 1, :] = jnp.sum(prob * shifted, axis=0, keepdims=True)
        stats[3, i : i + 1, :] = jnp.sum(prob, axis=0, keepdims=True)


def scores(scale, users, items, probs):
    cols, places = len(users), len(items)
    rows, width = users[0].shape
    return pl.pallas_call(
        functools.partial(score_body, cols, places, scale),
        in_specs=[VMEM] * (2 * cols + places),
        out_specs=[VMEM, VMEM],
        out_shape=[
            struct((places * rows, cols * rows), jnp.float32),
            struct((4, cols, rows), jnp.float32),
        ],
        scratch_shapes=[pltpu.VMEM((cols * rows, width), jnp.bfloat16), pltpu.VMEM((2 * rows, width), jnp.bfloat16)],
        compiler_params=params(32),
        cost_estimate=cost(2 * cols * places * rows * rows * width, 8 * cols * places * rows * rows),
    )(*users, *items, *probs)


def far_body(cols, places, factor, entropy, *refs):
    stats, users, probs = refs[:cols], refs[cols : 2 * cols], refs[2 * cols : 3 * cols]
    weights, grads, divergence, far = refs[3 * cols : 3 * cols + 4]
    all_users = refs[3 * cols + 4]
    rows = users[0].shape[0]
    lay(users, all_users)
    for i in range(cols):
        tops = [stats[j][0, i ^ j : (i ^ j) + 1, :] for j in range(cols)]
        sums = [stats[j][1, i ^ j : (i ^ j) + 1, :] for j in range(cols)]
        top = functools.reduce(jnp.maximum, tops)
        norm = functools.reduce(jnp.add, [s * jnp.exp(t - top) for s, t in zip(sums, tops)])
        ratio = jnp.exp(tops[0] - top) / norm
        if i == 0:
            lse = top + jnp.log(norm)
            terms = [stats[j][3, j : j + 1, :] * (lse - tops[j]) - stats[j][2, j : j + 1, :] for j in range(cols)]
            divergence[...] = functools.reduce(jnp.add, terms, entropy[...])
        prob = jnp.maximum(probs[i][...].reshape(places * rows, rows), 0.0)
        lanes = slice(i * rows, (i + 1) * rows)
        grads[:, lanes] = (factor * (weights[:, lanes] * ratio - prob)).astype(jnp.bfloat16)
    half = places * rows // CORES
    far[...] = jnp.dot(grads[half:], all_users[...], preferred_element_type=jnp.float32).astype(far.dtype)


def far_parts(factor, entropy, stats, users, probs, weights):
    cols, places = len(users), probs[0].shape[0]
    rows, width = users[0].shape
    return pl.pallas_call(
        functools.partial(far_body, cols, places, factor),
        in_specs=[VMEM] * (2 + 3 * cols),
        out_specs=[VMEM] * 3,
        out_shape=[
            struct(weights.shape, jnp.bfloat16),
            struct((1, rows), jnp.float32),
            struct((places * rows // CORES, width), jnp.bfloat16),
        ],
        scratch_shapes=[pltpu.VMEM((cols * rows, width), jnp.bfloat16)],
        compiler_params=params(32),
        cost_estimate=cost(cols * places * rows * rows * width, 8 * cols * places * rows * rows),
    )(entropy, *stats, *users, *probs, weights)


def near_body(cols, grads, *refs):
    users, (near, all_users) = refs[:cols], refs[cols:]
    lay(users, all_users)
    near[...] = jnp.dot(grads[: near.shape[0]], all_users[...], preferred_element_type=jnp.float32)


def near_part(grads, users):
    cols, places = len(users), grads.shape[0]
    rows, width = users[0].shape
    return pl.pallas_call(
        functools.partial(near_body, cols),
        in_specs=[VMEM] * (1 + cols),
        out_specs=VMEM,
        out_shape=struct((places // CORES, width), jnp.float32),
        scratch_shapes=[pltpu.VMEM((cols * rows, width), jnp.bfloat16)],
        compiler_params=params(32),
        cost_estimate=cost(grads.size * width, 4 * grads.size),
    )(grads, *users)


def user_body(cols, places, grads, *refs):
    items, refs = refs[:places], refs[-cols - 1 :]
    parts, all_items = refs[:cols], refs[cols]
    rows = items[0].shape[0]
    lay(items, all_items)
    for i in range(cols - 1, -1, -1):
        part = lax.dot_general(
            grads[:, i * rows : (i + 1) * rows],
            all_items[...],
            (((0,), (0,)), ((), ())),
            preferred_element_type=jnp.float32,
        )
        parts[i][...] = part.astype(parts[i].dtype)


def user_parts(cols, grads, items, after):
    places = len(items)
    rows, width = items[0].shape
    return pl.pallas_call(
        functools.partial(user_body, cols, places),
        in_specs=[VMEM] * (1 + places) + [ANY] * len(after),
        out_specs=[VMEM] * cols,
        out_shape=[struct((rows, width), jnp.bfloat16 if i else jnp.float32) for i in range(cols)],
        scratch_shapes=[pltpu.VMEM((places * rows, width), jnp.bfloat16)],
        compiler_params=params(32),
        cost_estimate=cost(2 * grads.size * width, 4 * grads.size),
    )(grads, *items, *after)


def join_body(planes, near, far, *outs):
    rows = outs[0].shape[0]
    for i in range(planes - 1, -1, -1):
        part = slice(i * rows, (i + 1) * rows)
        outs[i][...] = (near[part] + far[part].astype(jnp.float32)).astype(outs[i].dtype)


def join(planes, near, far):
    rows, width = near.shape[0] // planes, near.shape[1]
    return pl.pallas_call(
        functools.partial(join_body, planes),
        in_specs=[VMEM, VMEM],
        out_specs=[VMEM] * planes,
        out_shape=[struct((rows, width), jnp.bfloat16 if i % 2 else jnp.float32) for i in range(planes)],
        compiler_params=params(24),
        cost_estimate=cost(near.size, 8 * near.size),
    )(near, far)


def shards(
    user_feats, item_feats, user_w_in, user_w_out, item_w_in, item_w_out, teacher, cand_blocks, cand_count, owner_map
):
    rows, width = user_feats.shape
    slots = cand_blocks.shape[1]
    count = lax.axis_size("dp")
    cols = 1 << ((count // CORES).bit_length() - 1) // 2
    planes = count // (CORES * cols)
    assert cols * planes * CORES == count and count & (count - 1) == 0
    scale = 3.0 / math.sqrt(width)
    factor = rows * slots / 4.0 * scale
    me = lax.axis_index("dp").reshape(1).astype(jnp.int32)

    def swap(array, apart):
        return lax.ppermute(array, "dp", [(i, i ^ apart) for i in range(count)])

    def over_columns(own):
        return [swap(own, c * CORES) for c in range(1, cols)]

    *probs, entropy = spread_teacher(cols, planes, me, cand_blocks, cand_count, owner_map, teacher)
    first, *rest = probs
    probs = [first] + [swap(part, (c + 1) * CORES) for c, part in enumerate(rest)]

    item_emb = embed(item_feats, item_w_in, item_w_out, [first], True)
    wide = planes // 2
    crossed = [swap(item_emb, z * cols * CORES) for z in range(wide, planes if planes > 1 else 0, max(wide, 1))]
    nearby = [swap(item_emb, z * cols * CORES) for z in range(1, wide)]
    user_emb = embed(user_feats, user_w_in, user_w_out, [item_emb], False)
    user_emb, item_emb, probs, crossed, nearby = lax.optimization_barrier((user_emb, item_emb, probs, crossed, nearby))
    users = [user_emb] + over_columns(user_emb)
    probs = turned(probs)
    item_emb, nearby, crossed, probs = lax.optimization_barrier((item_emb, nearby, crossed, probs))
    derived = [swap(block, z * cols * CORES) for block in crossed for z in range(1, wide)]
    items = [item_emb] + nearby + crossed + derived
    items = items + [swap(block, 1) for block in items]

    weights, stats = scores(scale, users, items, probs)
    grads, divergence, far = far_parts(factor, entropy, [stats] + over_columns(stats), users, probs, weights)
    far = swap(far, 1)
    parts = join(planes, near_part(grads, users), far)
    hop = cols * CORES
    if planes == 4:
        merged = (parts[2] + swap(parts[3], hop).astype(jnp.float32)).astype(jnp.bfloat16)
        sent = [swap(merged, 2 * hop), swap(parts[1], hop)]
    else:
        sent = [swap(parts[z].astype(jnp.bfloat16), z * hop) for z in range(planes - 1, 0, -1)]
    own, *others = user_parts(cols, grads, items, [parts[0]])
    arrived = [swap(part, (c + 1) * CORES) for c, part in enumerate(others)]

    def add(start, parts):
        return functools.reduce(jnp.add, [part.astype(jnp.float32) for part in parts], start)

    return (divergence.reshape(rows), add(own, arrived), add(parts[0], sent))


def solution(mesh):
    both = ("dp", "tensor")
    placed = (
        P(both, None),
        P(both, None),
        P(None, "tensor"),
        P("tensor", None),
        P(None, "tensor"),
        P("tensor", None),
        P(both, None),
        P(both, None),
        P(both),
        P(),
    )
    return jax.shard_map(
        shards,
        mesh=mesh,
        in_specs=placed,
        out_specs=(P(both), P(both, None), P(both, None)),
        check_vma=False,
    )
```

```python
import functools
import math

import jax
import jax.numpy as jnp
from jax import lax
from jax.experimental import pallas as pl
from jax.experimental.pallas import tpu as pltpu
from jax.sharding import PartitionSpec as P

CORES = 2
LOWEST = -1e30
DEAD = -1.0
MIB = 1 << 20
ANY = pl.BlockSpec(memory_space=pl.ANY)
VMEM = pl.BlockSpec(memory_space=pltpu.VMEM)
SMEM = pl.BlockSpec(memory_space=pltpu.SMEM)


def struct(shape, dtype):
    return jax.ShapeDtypeStruct(shape, dtype)


def params(mib):
    return pltpu.CompilerParams(vmem_limit_bytes=mib * MIB)


def cost(flops, moved):
    return pl.CostEstimate(flops=int(flops), bytes_accessed=int(moved), transcendentals=0)


def in_hbm(array):
    return pltpu.with_memory_space_constraint(array, pltpu.HBM)


def tower_body(chunks, ready, feats, w_in, w_out, *refs):
    out, held_out, total, sem_out, *own = refs[-4 if ready else -6 :]
    step = w_in.shape[1] // chunks

    def part(i):
        return pl.ds(pl.multiple_of(i * step, step), step)

    def copies(i):
        both = [pltpu.make_async_copy(w_out.at[part(i)], held_out.at[part(i)], sem_out.at[i])]
        if not ready:
            both.insert(0, pltpu.make_async_copy(w_in.at[:, part(i)], own[0].at[:, part(i)], own[1].at[i]))
        return both

    for i in range(chunks):
        for copy in copies(i):
            copy.start()
    total[...] = jnp.zeros_like(total)
    held_in = w_in if ready else own[0]

    def one(i, carry):
        waits = copies(i)
        if not ready:
            waits[0].wait()
        hidden = jnp.dot(feats[...], held_in[:, part(i)], preferred_element_type=jnp.float32)
        hidden = jnp.maximum(hidden, 0.0).astype(jnp.bfloat16)
        waits[-1].wait()
        total[...] += jnp.dot(hidden, held_out[part(i)], preferred_element_type=jnp.float32)
        return carry

    lax.fori_loop(0, chunks, one, 0, unroll=True)
    out[...] = total[...].astype(out.dtype)


def tower(feats, w_in, w_out, dtype, after, ready):
    rows, width = feats.shape
    hidden = w_in.shape[1]
    chunks = max(1, hidden // (2048 if ready else 1024))
    own = [] if ready else [pltpu.VMEM(w_in.shape, w_in.dtype), pltpu.SemaphoreType.DMA((chunks,))]
    return pl.pallas_call(
        functools.partial(tower_body, chunks, ready),
        in_specs=[VMEM, VMEM if ready else ANY, ANY] + [ANY] * len(after),
        out_specs=VMEM,
        out_shape=struct((rows, width), dtype),
        scratch_shapes=[
            pltpu.VMEM(w_out.shape, w_out.dtype),
            pltpu.VMEM((rows, width), jnp.float32),
            pltpu.SemaphoreType.DMA((chunks,)),
        ]
        + own,
        compiler_params=params(20 if ready else 52),
        cost_estimate=cost(1, 1),
    )(feats, w_in if ready else in_hbm(w_in), in_hbm(w_out), *after)


def embed(feats, w_in, w_out, after, ready):
    if lax.axis_size("tensor") == 1:
        return tower(feats, w_in, w_out, jnp.bfloat16, after, ready)
    feats = lax.all_gather(feats, "tensor", axis=0, tiled=True)
    partial = tower(feats, w_in, w_out, jnp.float32, after, ready)
    return lax.psum_scatter(partial, "tensor", scatter_dimension=0, tiled=True).astype(jnp.bfloat16)


def teacher_body(cols, planes, me, cands_hbm, count, owner_hbm, teacher_hbm, *refs):
    outs, (entropy, dense, sems, teacher, cands, owner, load_sems) = refs[:cols], refs[cols:]
    loads = [
        pltpu.make_async_copy(source, target, load_sems.at[i])
        for i, (source, target) in enumerate([(teacher_hbm, teacher), (cands_hbm, cands), (owner_hbm, owner)])
    ]
    for copy in loads:
        copy.start()
    dense[...] = jnp.full(dense.shape, DEAD, jnp.float32)
    for copy in loads:
        copy.wait()
    rows = teacher.shape[0]
    slots = cands.shape[1]
    live = count[0]
    logits = teacher[...]
    usable = lax.broadcasted_iota(jnp.int32, logits.shape, 1) < live * rows
    shifted = logits - jnp.max(jnp.where(usable, logits, -jnp.inf), axis=1, keepdims=True)
    weight = jnp.where(usable, jnp.exp(shifted), 0.0)
    norm = jnp.sum(weight, axis=1, keepdims=True)
    prob = weight / norm
    log_sum = jnp.sum(jnp.where(usable, prob * (shifted - jnp.log(norm)), 0.0), axis=1, keepdims=True)
    entropy[...] = jnp.broadcast_to(log_sum, (rows, rows)).T[:1]
    for k in range(slots):

        @pl.when(k < live)
        def _():
            apart = owner[cands[0, k]] ^ me[0]
            inside = apart % (CORES * cols)
            place = (inside % CORES) * planes + apart // (CORES * cols)
            dense[inside // CORES, place] = prob[:, k * rows : (k + 1) * rows]

    copies = [pltpu.make_async_copy(dense.at[i], outs[i], sems.at[i]) for i in range(cols)]
    for copy in copies:
        copy.start()
    for copy in copies:
        copy.wait()


def spread_teacher(cols, planes, me, cands, count, owner, teacher):
    rows = teacher.shape[0]
    places = CORES * planes
    return pl.pallas_call(
        functools.partial(teacher_body, cols, planes),
        in_specs=[SMEM, ANY, SMEM, ANY, ANY],
        out_specs=[ANY] * cols + [VMEM],
        out_shape=[struct((places, rows, rows), jnp.float32)] * cols + [struct((1, rows), jnp.float32)],
        scratch_shapes=[
            pltpu.VMEM((cols, places, rows, rows), jnp.float32),
            pltpu.SemaphoreType.DMA((cols,)),
            pltpu.VMEM(teacher.shape, teacher.dtype),
            pltpu.SMEM(cands.shape, cands.dtype),
            pltpu.SMEM(owner.shape, owner.dtype),
            pltpu.SemaphoreType.DMA((3,)),
        ],
        compiler_params=params(24),
        cost_estimate=cost(10**10, 8 * teacher.size),
    )(me, in_hbm(cands), count, in_hbm(owner), in_hbm(teacher))


def turn_body(cols, *refs):
    for source, out in zip(refs[:cols], refs[cols:]):
        for i in range(source.shape[0]):
            out[i] = source[i].T


def turned(probs):
    return pl.pallas_call(
        functools.partial(turn_body, len(probs)),
        in_specs=[VMEM] * len(probs),
        out_specs=[VMEM] * len(probs),
        out_shape=[struct(part.shape, part.dtype) for part in probs],
        compiler_params=params(24),
        cost_estimate=cost(1, 1),
    )(*probs)


def lay(sources, target):
    rows = sources[0].shape[0]
    for i, source in enumerate(sources):
        target[i * rows : (i + 1) * rows] = source[...]


def score_body(cols, places, scale, *refs):
    users, items, probs = refs[:cols], refs[cols : cols + places], refs[cols + places : 2 * cols + places]
    weights, stats, all_users, all_items = refs[2 * cols + places :]
    rows = users[0].shape[0]
    lay(users, all_users)
    step = 2 if places % 2 == 0 else 1
    for first in range(0, places, step):
        lay(items[first : first + step], all_items)
        weights[first * rows : (first + step) * rows] = scale * lax.dot_general(
            all_items[: step * rows], all_users[...], (((1,), (1,)), ((), ())), preferred_element_type=jnp.float32
        )
    for i in range(cols):
        lanes = slice(i * rows, (i + 1) * rows)
        score = weights[:, lanes]
        prob = probs[i][...].reshape(places * rows, rows)
        live = prob >= 0.0
        prob = jnp.maximum(prob, 0.0)
        top = jnp.max(jnp.where(live, score, LOWEST), axis=0, keepdims=True)
        shifted = jnp.where(live, score - top, 0.0)
        weight = jnp.where(live, jnp.exp(shifted), 0.0)
        weights[:, lanes] = weight
        stats[0, i : i + 1, :] = top
        stats[1, i : i + 1, :] = jnp.sum(weight, axis=0, keepdims=True)
        stats[2, i : i + 1, :] = jnp.sum(prob * shifted, axis=0, keepdims=True)
        stats[3, i : i + 1, :] = jnp.sum(prob, axis=0, keepdims=True)


def scores(scale, users, items, probs):
    cols, places = len(users), len(items)
    rows, width = users[0].shape
    return pl.pallas_call(
        functools.partial(score_body, cols, places, scale),
        in_specs=[VMEM] * (2 * cols + places),
        out_specs=[VMEM, VMEM],
        out_shape=[
            struct((places * rows, cols * rows), jnp.float32),
            struct((4, cols, rows), jnp.float32),
        ],
        scratch_shapes=[pltpu.VMEM((cols * rows, width), jnp.bfloat16), pltpu.VMEM((2 * rows, width), jnp.bfloat16)],
        compiler_params=params(32),
        cost_estimate=cost(2 * cols * places * rows * rows * width, 8 * cols * places * rows * rows),
    )(*users, *items, *probs)


def far_body(cols, places, factor, entropy, *refs):
    stats, users, probs = refs[:cols], refs[cols : 2 * cols], refs[2 * cols : 3 * cols]
    weights, grads, divergence, ratios, far, all_users = refs[3 * cols :]
    half = places * users[0].shape[0] // CORES
    rows = users[0].shape[0]
    lay(users, all_users)
    for i in range(cols):
        tops = [stats[j][0, i ^ j : (i ^ j) + 1, :] for j in range(cols)]
        sums = [stats[j][1, i ^ j : (i ^ j) + 1, :] for j in range(cols)]
        top = functools.reduce(jnp.maximum, tops)
        norm = functools.reduce(jnp.add, [s * jnp.exp(t - top) for s, t in zip(sums, tops)])
        ratio = jnp.exp(tops[0] - top) / norm
        if i == 0:
            lse = top + jnp.log(norm)
            terms = [stats[j][3, j : j + 1, :] * (lse - tops[j]) - stats[j][2, j : j + 1, :] for j in range(cols)]
            divergence[...] = functools.reduce(jnp.add, terms, entropy[...])
        ratios[i : i + 1, :] = ratio
        prob = jnp.maximum(probs[i][places // CORES :].reshape(half, rows), 0.0)
        lanes = slice(i * rows, (i + 1) * rows)
        grads[:, lanes] = (factor * (weights[half:, lanes] * ratio - prob)).astype(jnp.bfloat16)
    far[...] = jnp.dot(grads[...], all_users[...], preferred_element_type=jnp.float32).astype(far.dtype)


def far_parts(factor, entropy, stats, users, probs, weights):
    cols, places = len(users), probs[0].shape[0]
    rows, width = users[0].shape
    return pl.pallas_call(
        functools.partial(far_body, cols, places, factor),
        in_specs=[VMEM] * (2 + 3 * cols),
        out_specs=[VMEM] * 4,
        out_shape=[
            struct((places * rows // CORES, cols * rows), jnp.bfloat16),
            struct((1, rows), jnp.float32),
            struct((cols, rows), jnp.float32),
            struct((places * rows // CORES, width), jnp.bfloat16),
        ],
        scratch_shapes=[pltpu.VMEM((cols * rows, width), jnp.bfloat16)],
        compiler_params=params(32),
        cost_estimate=cost(cols * places * rows * rows * width, 8 * cols * places * rows * rows),
    )(entropy, *stats, *users, *probs, weights)


def near_body(cols, places, factor, ratios, weights, *refs):
    users, probs, (near, grads, all_users) = refs[:cols], refs[cols : 2 * cols], refs[2 * cols :]
    rows = users[0].shape[0]
    half = near.shape[0]
    lay(users, all_users)
    for i in range(cols):
        prob = jnp.maximum(probs[i][: places // CORES].reshape(half, rows), 0.0)
        lanes = slice(i * rows, (i + 1) * rows)
        grads[:, lanes] = (factor * (weights[:half, lanes] * ratios[i : i + 1, :] - prob)).astype(jnp.bfloat16)
    near[...] = jnp.dot(grads[...], all_users[...], preferred_element_type=jnp.float32)


def near_part(factor, ratios, weights, users, probs):
    cols, places = len(users), probs[0].shape[0]
    rows, width = users[0].shape
    half = places * rows // CORES
    return pl.pallas_call(
        functools.partial(near_body, cols, places, factor),
        in_specs=[VMEM] * (2 + 2 * cols),
        out_specs=[VMEM] * 2,
        out_shape=[struct((half, width), jnp.float32), struct((half, cols * rows), jnp.bfloat16)],
        scratch_shapes=[pltpu.VMEM((cols * rows, width), jnp.bfloat16)],
        compiler_params=params(32),
        cost_estimate=cost(weights.size * width, 4 * weights.size),
    )(ratios, weights, *users, *probs)


def user_body(cols, places, near, far, *refs):
    items, refs = refs[:places], refs[-cols - 1 :]
    parts, all_items = refs[:cols], refs[cols]
    rows = items[0].shape[0]
    lay(items, all_items)
    for i in range(cols - 1, -1, -1):
        part = functools.reduce(
            jnp.add,
            [
                lax.dot_general(
                    grads[:, i * rows : (i + 1) * rows],
                    all_items[h * grads.shape[0] : (h + 1) * grads.shape[0]],
                    (((0,), (0,)), ((), ())),
                    preferred_element_type=jnp.float32,
                )
                for h, grads in enumerate((near, far))
            ],
        )
        parts[i][...] = part.astype(parts[i].dtype)


def user_parts(cols, near, far, items, after):
    places = len(items)
    rows, width = items[0].shape
    return pl.pallas_call(
        functools.partial(user_body, cols, places),
        in_specs=[VMEM] * (2 + places) + [ANY] * len(after),
        out_specs=[VMEM] * cols,
        out_shape=[struct((rows, width), jnp.bfloat16 if i else jnp.float32) for i in range(cols)],
        scratch_shapes=[pltpu.VMEM((places * rows, width), jnp.bfloat16)],
        compiler_params=params(32),
        cost_estimate=cost(4 * near.size * width, 8 * near.size),
    )(near, far, *items, *after)


def join_body(planes, near, far, *outs):
    rows = outs[0].shape[0]
    for i in range(planes - 1, -1, -1):
        part = slice(i * rows, (i + 1) * rows)
        outs[i][...] = (near[part] + far[part].astype(jnp.float32)).astype(outs[i].dtype)


def join(planes, near, far):
    rows, width = near.shape[0] // planes, near.shape[1]
    return pl.pallas_call(
        functools.partial(join_body, planes),
        in_specs=[VMEM, VMEM],
        out_specs=[VMEM] * planes,
        out_shape=[struct((rows, width), jnp.bfloat16 if i % 2 else jnp.float32) for i in range(planes)],
        compiler_params=params(24),
        cost_estimate=cost(near.size, 8 * near.size),
    )(near, far)


def shards(
    user_feats, item_feats, user_w_in, user_w_out, item_w_in, item_w_out, teacher, cand_blocks, cand_count, owner_map
):
    rows, width = user_feats.shape
    slots = cand_blocks.shape[1]
    count = lax.axis_size("dp")
    cols = 1 << ((count // CORES).bit_length() - 1) // 2
    planes = count // (CORES * cols)
    assert cols * planes * CORES == count and count & (count - 1) == 0
    scale = 3.0 / math.sqrt(width)
    factor = rows * slots / 4.0 * scale
    me = lax.axis_index("dp").reshape(1).astype(jnp.int32)

    def swap(array, apart):
        return lax.ppermute(array, "dp", [(i, i ^ apart) for i in range(count)])

    def over_columns(own):
        return [swap(own, c * CORES) for c in range(1, cols)]

    *probs, entropy = spread_teacher(cols, planes, me, cand_blocks, cand_count, owner_map, teacher)
    first, *rest = probs
    probs = [first] + [swap(part, (c + 1) * CORES) for c, part in enumerate(rest)]

    item_emb = embed(item_feats, item_w_in, item_w_out, [first], True)
    wide = planes // 2
    crossed = [swap(item_emb, z * cols * CORES) for z in range(wide, planes if planes > 1 else 0, max(wide, 1))]
    nearby = [swap(item_emb, z * cols * CORES) for z in range(1, wide)]
    user_emb = embed(user_feats, user_w_in, user_w_out, [item_emb], False)
    user_emb, item_emb, probs, crossed, nearby = lax.optimization_barrier((user_emb, item_emb, probs, crossed, nearby))
    users = [user_emb] + over_columns(user_emb)
    probs = turned(probs)
    item_emb, nearby, crossed, probs = lax.optimization_barrier((item_emb, nearby, crossed, probs))
    derived = [swap(block, z * cols * CORES) for block in crossed for z in range(1, wide)]
    items = [item_emb] + nearby + crossed + derived
    items = items + [swap(block, 1) for block in items]

    weights, stats = scores(scale, users, items, probs)
    grads_far, divergence, ratios, far = far_parts(factor, entropy, [stats] + over_columns(stats), users, probs, weights)
    far = swap(far, 1)
    near, grads_near = near_part(factor, ratios, weights, users, probs)
    parts = join(planes, near, far)
    hop = cols * CORES
    if planes == 4:
        merged = (parts[2] + swap(parts[3], hop).astype(jnp.float32)).astype(jnp.bfloat16)
        sent = [swap(merged, 2 * hop), swap(parts[1], hop)]
    else:
        sent = [swap(parts[z].astype(jnp.bfloat16), z * hop) for z in range(planes - 1, 0, -1)]
    own, *others = user_parts(cols, grads_near, grads_far, items, [parts[0]])
    arrived = [swap(part, (c + 1) * CORES) for c, part in enumerate(others)]

    def add(start, parts):
        return functools.reduce(jnp.add, [part.astype(jnp.float32) for part in parts], start)

    return (divergence.reshape(rows), add(own, arrived), add(parts[0], sent))


def solution(mesh):
    both = ("dp", "tensor")
    placed = (
        P(both, None),
        P(both, None),
        P(None, "tensor"),
        P("tensor", None),
        P(None, "tensor"),
        P("tensor", None),
        P(both, None),
        P(both, None),
        P(both),
        P(),
    )
    return jax.shard_map(
        shards,
        mesh=mesh,
        in_specs=placed,
        out_specs=(P(both), P(both, None), P(both, None)),
        check_vma=False,
    )
```
